256 devices in a mesh: gx: 32 (over z, y), gy: 2 (over core), gz: 4 (over x).
Axes of the slice: x: 4, y: 4, z: 8, core: 2. Of those that a mesh axis runs over, the one named last changes fastest.
Arguments:
- snapshot: float32 [1024, 512, 512], P('gx', 'gy', 'gz'), may hold values from -6 to 6
- factor_x: float32 [1024, 128], P('gx'), may hold values from -0.375 to 0.375
- factor_y: float32 [512, 128], P('gy'), may hold values from -0.375 to 0.375
- factor_z: float32 [512, 128], P('gz'), may hold values from -0.375 to 0.375
Outputs:
- core: float32 [128, 128, 128], P('gx', 'gy', 'gz')
The draws below stay inside these ranges and needn't reach their ends.
All inputs are finite; a program needn't handle non-finite values.
Results may differ from the reference program's by a relative error of at most 0.00007.
Values sent between devices are 32-bit elements; how exact they have to be, the bound alone decides.
A program may use at most 64 MiB of HBM per device.

```python
import jax
import jax.numpy as jnp
from jax import lax

R = 128
NX = 1024
NY = 512
NZ = 512


def with_spikes(result, stream_key, source, target, shards_of, factor):
    def block_of(axis_at):
        return (jnp.arange(result.shape[axis_at]) // (result.shape[axis_at] // shards_of)).reshape((-1,) + (1,) * (result.ndim - 1 - axis_at))

    near = jax.random.permutation(stream_key, shards_of)[block_of(target)]
    second = (block_of(target) + shards_of // 2) % shards_of
    return jnp.where((block_of(source) == near) | (block_of(source) == second), factor * result, result)


def steps_of(rng, shape, split, least, largest):
    gain, own = 1.0, jax.random.fold_in(rng, 6)
    for axis_at, parts in split:
        heights = jnp.exp(jax.random.uniform(jax.random.fold_in(own, axis_at), (parts,), jnp.float32, least / len(split), largest / len(split)))
        gain = gain * jnp.repeat(heights, shape[axis_at] // parts).reshape([-1 if axis == axis_at else 1 for axis in range(len(shape))])
    return gain


def normal_values(own_key, shape, spread, bound, split=(), kind=jnp.bfloat16):
    level = steps_of(own_key, shape, split, -0.22, 0.18) if split else 1.0
    array = jax.random.normal(own_key, shape, jnp.float32) * spread * level
    return jnp.minimum(jnp.maximum(array, -bound), bound).astype(kind)


def gaussian_with(key, extent, spread, most, cuts, heavy, dtype=jnp.bfloat16):
    result = spread * jax.random.normal(key, extent, jnp.float32)
    if cuts:
        result = result * steps_of(key, extent, cuts, -0.22, 0.18)
    return jnp.clip(with_spikes(result, jax.random.fold_in(key, 3), *heavy), -most, most).astype(dtype)


def setup_inputs(seed: int = 0) -> dict:
    key_of = jax.random.split(jax.random.key(seed), 5)
    return {
        "snapshot": normal_values(key_of[0], (NX, NY, NZ), 1.0, 6.0, ((0, 32), (1, 2), (2, 4)), jnp.float32),
        "factor_x": gaussian_with(key_of[1], (NX, R), NX ** -0.5, 0.375, ((0, 32),), (0, 1, 32, 2.75), jnp.float32),
        "factor_y": gaussian_with(key_of[2], (NY, R), NY ** -0.5, 0.375, ((0, 2),), (0, 1, 2, 2.0), jnp.float32),
        "factor_z": gaussian_with(key_of[3], (NZ, R), NZ ** -0.5, 0.375, ((0, 4),), (0, 1, 4, 2.0), jnp.float32),
    }


def reference(snapshot, factor_x, factor_y, factor_z):
    highest = lax.Precision.HIGHEST
    first = jnp.einsum("xyz,xa->ayz", snapshot, factor_x, precision=highest)
    second = jnp.einsum("ayz,yb->abz", first, factor_y, precision=highest)
    return jnp.einsum("abz,zc->abc", second, factor_z, precision=highest)
```

```python
import functools

import jax
import jax.numpy as jnp
from jax import lax
from jax.experimental import pallas as pl
from jax.experimental.pallas import tpu as pltpu
from jax.sharding import PartitionSpec as P

MESH = pl.DeviceIdType.MESH
F32, BF16 = jnp.float32, jnp.bfloat16
NT = (((1,), (1,)), ((), ()))
CHUNKS = 4


def split(value):
    high = value.astype(BF16)
    return high, (value - high.astype(F32)).astype(BF16)


def rows(start, size):
    return pl.ds(pl.multiple_of(start, 8), size)


def stacked(factor_t):
    high, low = split(factor_t)
    top = jnp.concatenate([high, high], axis=1)
    return jnp.concatenate([top, jnp.concatenate([low, jnp.zeros_like(low)], axis=1)], axis=0)


def kernel(
    zn, snap, fx, fy, fz, out,
    s_buf, fy_v, fz_v, fyl, fzl, fxl, fxg, t1s, t1r, t3, rx1, rx2, v, r, p, zr, fs, fr,
    s_sem, f_sem, ys, yr, s1, r1, s2, r2, a_s, a_r, z_s, z_r, e_s, e_r, g_s, g_r,
):
    gx, core, xi = lax.axis_index("gx"), lax.axis_index("gy"), lax.axis_index("gz")
    zi, yi = gx // 4, lax.rem(gx, 4)
    me = yi * 2 + core
    other = 1 - core
    right, opposite, left = lax.rem(xi + 1, 4), lax.rem(xi + 2, 4), lax.rem(xi + 3, 4)

    def group(d):
        m = lax.rem(me + d, 8)
        return m, (zi * 4 + m // 2, lax.rem(m, 2), xi)

    def ring(d):
        z = lax.rem(zi + d, zn)
        return z, (z * 4 + yi, core, xi)

    def load(i):
        x = jnp.where(i < 8, other * 16 + 2 * i, core * 16 + 2 * i - 16)
        return pltpu.make_async_copy(snap.at[pl.ds(x, 2)], s_buf.at[i], s_sem.at[i])

    load_y = pltpu.make_async_copy(fy, fy_v, f_sem.at[0])
    load_z = pltpu.make_async_copy(fz, fz_v, f_sem.at[1])
    my_fx = fxg.at[rows(yi * 32, 32)]
    load_x = pltpu.make_async_copy(fx, my_fx, f_sem.at[2])
    load_y.start()

    @pl.loop(0, 16)
    def _(i):
        load(i).start()

    load_z.start()
    load_x.start()

    barrier = pltpu.get_barrier_semaphore()

    @pl.loop(1, 8)
    def _(d):
        pl.semaphore_signal(barrier, inc=1, device_id=group(d)[1], device_id_type=MESH)

    @pl.loop(1, zn)
    def _(d):
        pl.semaphore_signal(barrier, inc=1, device_id=ring(d)[1], device_id_type=MESH)

    for x in (left, right):
        pl.semaphore_signal(barrier, inc=1, device_id=(gx, core, x), device_id_type=MESH)

    load_y.wait()
    high, low = split(fy_v[...].T)
    fyl[...] = jnp.concatenate([high, low], axis=0)
    load_z.wait()
    fzl[...] = stacked(fz_v[...].T)
    load_x.wait()
    pl.semaphore_wait(barrier, 7 + (zn - 1) + 2)

    def gather_fx(d):
        y = lax.rem(yi + d, 4)
        return pltpu.make_async_remote_copy(
            src_ref=my_fx, dst_ref=my_fx, send_sem=g_s, recv_sem=g_r,
            device_id=(zi * 4 + y, core, xi), device_id_type=MESH)

    @pl.loop(1, 4)
    def _(d):
        gather_fx(d).start()

    def first_of(i):
        load(i).wait()
        s = jnp.concatenate([s_buf[i, 0], s_buf[i, 1]], axis=1)
        high, low = split(s)
        both = jnp.dot(fyl[...], high, preferred_element_type=F32)
        rest = jnp.dot(fyl[0:128], low, preferred_element_type=F32)
        return both[:128] + both[128:] + rest

    def swap(i):
        return pltpu.make_async_remote_copy(
            src_ref=t1s.at[i], dst_ref=t1r.at[i], send_sem=ys.at[i], recv_sem=yr.at[i],
            device_id=(gx, other, xi), device_id_type=MESH)

    @pl.loop(0, 8)
    def _(i):
        t = first_of(i)
        t1s[i, 0] = t[:, :128]
        t1s[i, 1] = t[:, 128:]
        swap(i).start()

    @pl.loop(0, 8)
    def _(i):
        t = first_of(8 + i)
        swap(i).wait_recv()
        t2 = jnp.concatenate([t[:, :128] + t1r[i, 0], t[:, 128:] + t1r[i, 1]], axis=0)
        w = jnp.concatenate(split(t2), axis=1)
        q = lax.dot_general(fzl[...], w, NT, preferred_element_type=F32)
        q = q[:128] + q[128:]
        t3[pl.ds(2 * i, 128, stride=16), :] = q[:, :128]
        t3[pl.ds(2 * i + 1, 128, stride=16), :] = q[:, 128:]

    def opposite_part(k, way):
        src = t3.at[rows(opposite * 512 + k * 128 + way * 64, 64)]
        return pltpu.make_async_remote_copy(
            src_ref=src, dst_ref=rx1.at[way, k], send_sem=s1.at[way, k], recv_sem=r1.at[way, k],
            device_id=(gx, core, (right, left)[way]), device_id_type=MESH)

    def next_part(k, way):
        to = (right, left)[way]
        return pltpu.make_async_remote_copy(
            src_ref=t3.at[rows(to * 512 + k * 128, 128)], dst_ref=rx2.at[way, k],
            send_sem=s2.at[way, k], recv_sem=r2.at[way, k],
            device_id=(gx, core, to), device_id_type=MESH)

    def exchange(k, d):
        m, to = group(d)
        return pltpu.make_async_remote_copy(
            src_ref=v.at[k, rows(m * 16, 16)], dst_ref=r.at[k, rows(me * 16, 16)],
            send_sem=a_s.at[k], recv_sem=a_r.at[k], device_id=to, device_id_type=MESH)

    def spread(k, d):
        z, to = ring(d)
        return pltpu.make_async_remote_copy(
            src_ref=p.at[k, rows(z * 16, 16)], dst_ref=zr.at[k, d - 1],
            send_sem=z_s.at[k], recv_sem=z_r.at[k], device_id=to, device_id_type=MESH)

    def finish(d):
        m, to = group(d)
        return pltpu.make_async_remote_copy(
            src_ref=fs.at[m // 2], dst_ref=fr.at[rows(me * 16, 16)],
            send_sem=e_s, recv_sem=e_r, device_id=to, device_id_type=MESH)

    def m1(k):
        for way in range(2):
            opposite_part(k, way).start()

    def m2(k):
        for way in range(2):
            opposite_part(k, way).wait_recv()
            part = rows((right, left)[way] * 512 + k * 128 + way * 64, 64)
            t3[part] = t3[part] + rx1[way, k]
            next_part(k, way).start()

    def gather(k):
        for way in range(2):
            next_part(k, way).wait_recv()
        v[k] = t3[rows(xi * 512 + k * 128, 128)] + rx2[0, k] + rx2[1, k]

        @pl.loop(1, 8)
        def _(d):
            exchange(k, d).start()

        r[k, rows(me * 16, 16)] = v[k, rows(me * 16, 16)]

    def contract(k):
        pltpu.make_async_copy(r.at[k, 0:112], r.at[k, 0:112], a_r.at[k]).wait()
        w = jnp.concatenate(split(r[k]), axis=0)
        q = jnp.dot(fxl[...], w, preferred_element_type=F32)
        p[k] = q[:128] + q[128:]

        @pl.loop(1, zn)
        def _(d):
            spread(k, d).start()

    def total(k):
        pltpu.make_async_copy(zr.at[k], zr.at[k], z_r.at[k]).wait()
        w = p[k, rows(zi * 16, 16)]
        for d in range(zn - 1):
            w = w + zr[k, d]
        for y in range(4):
            fs[y, 4 * k:4 * k + 4] = w[4 * y:4 * y + 4]

    m1(0)
    m1(1)
    pltpu.make_async_copy(fxg.at[0:96], fxg.at[0:96], g_r).wait()
    fxl[...] = stacked(fxg[...].T)
    for step in range(CHUNKS + 3):
        if step < CHUNKS:
            m2(step)
        if step + 2 < CHUNKS:
            m1(step + 2)
        if 0 <= step - 1 < CHUNKS:
            gather(step - 1)
        if 0 <= step - 2 < CHUNKS:
            contract(step - 2)
        if 0 <= step - 3 < CHUNKS:
            total(step - 3)

    @pl.loop(1, 8)
    def _(d):
        finish(d).start()

    fr[rows(me * 16, 16)] = fs[yi]
    pltpu.make_async_copy(fr.at[0:112], fr.at[0:112], e_r).wait()
    for a in range(4):
        c_b = jnp.concatenate([fr[pl.ds(4 * k + a, 8, stride=16), :] for k in range(CHUNKS)], axis=0)
        b_c = c_b.T
        out[a] = jnp.where(core == 0, b_c[:64], b_c[64:])

    @pl.loop(0, 8)
    def _(i):
        swap(i).wait_send()

    for k in range(CHUNKS):
        for way in range(2):
            opposite_part(k, way).wait_send()
            next_part(k, way).wait_send()
        pltpu.make_async_copy(v.at[k, 0:112], v.at[k, 0:112], a_s.at[k]).wait()
        pltpu.make_async_copy(zr.at[k], zr.at[k], z_s.at[k]).wait()
    pltpu.make_async_copy(fr.at[0:112], fr.at[0:112], e_s).wait()
    pltpu.make_async_copy(fxg.at[0:96], fxg.at[0:96], g_s).wait()


def body(zn, snapshot, factor_x, factor_y, factor_z):
    anywhere = pl.BlockSpec(memory_space=pl.ANY)
    dma = pltpu.SemaphoreType.DMA
    return pl.pallas_call(
        functools.partial(kernel, zn),
        out_shape=jax.ShapeDtypeStruct((4, 64, 32), F32),
        in_specs=[anywhere] * 4,
        out_specs=pl.BlockSpec(memory_space=pltpu.VMEM),
        scratch_shapes=[
            pltpu.VMEM((16, 2, 256, 128), F32),
            pltpu.VMEM((256, 128), F32),
            pltpu.VMEM((128, 128), F32),
            pltpu.VMEM((256, 256), BF16),
            pltpu.VMEM((256, 256), BF16),
            pltpu.VMEM((256, 256), BF16),
            pltpu.VMEM((128, 128), F32),
            pltpu.VMEM((8, 2, 128, 128), F32),
            pltpu.VMEM((8, 2, 128, 128), F32),
            pltpu.VMEM((2048, 128), F32),
            pltpu.VMEM((2, CHUNKS, 64, 128), F32),
            pltpu.VMEM((2, CHUNKS, 128, 128), F32),
            pltpu.VMEM((CHUNKS, 128, 128), F32),
            pltpu.VMEM((CHUNKS, 128, 128), F32),
            pltpu.VMEM((CHUNKS, 128, 128), F32),
            pltpu.VMEM((CHUNKS, zn - 1, 16, 128), F32),
            pltpu.VMEM((4, 16, 128), F32),
            pltpu.VMEM((128, 128), F32),
            dma((16,)), dma((3,)), dma((8,)), dma((8,)),
            dma((2, CHUNKS)), dma((2, CHUNKS)), dma((2, CHUNKS)), dma((2, CHUNKS)),
            dma((CHUNKS,)), dma((CHUNKS,)), dma((CHUNKS,)), dma((CHUNKS,)),
            dma, dma, dma, dma,
        ],
        compiler_params=pltpu.CompilerParams(
            collective_id=0, has_side_effects=True, vmem_limit_bytes=40 * 1024 * 1024
        ),
    )(snapshot, factor_x, factor_y, factor_z)


def solution(mesh):
    return jax.shard_map(
        functools.partial(body, mesh.shape["gx"] // 4),
        mesh=mesh,
        in_specs=(P("gx", "gy", "gz"), P("gx", None), P("gy", None), P("gz", None)),
        out_specs=P("gx", "gy", "gz"),
        check_vma=False,
    )
```

```python
import functools

import jax
import jax.numpy as jnp
from jax import lax
from jax.experimental import pallas as pl
from jax.experimental.pallas import tpu as pltpu
from jax.sharding import PartitionSpec as P

UNROLL = 1
MESH = pl.DeviceIdType.MESH
F32, BF16 = jnp.float32, jnp.bfloat16
NT = (((1,), (1,)), ((), ()))
CHUNKS = 2


def split(value):
    high = value.astype(BF16)
    return high, (value - high.astype(F32)).astype(BF16)


def rows(start, size):
    return pl.ds(pl.multiple_of(start, 8), size)


def stacked(factor_t):
    high, low = split(factor_t)
    top = jnp.concatenate([high, high], axis=1)
    return jnp.concatenate([top, jnp.concatenate([low, jnp.zeros_like(low)], axis=1)], axis=0)


def kernel(
    zn, snap, fx, fy, fz, out,
    s_buf, fy_v, fz_v, fxg, ft, fyl, fzl, fxl, t1s, t1o, t1r, t3, rx, p, zr, fin,
    s_sem, f_sem, ys, yr, x_s, x_r, z_s, z_r, g_s, g_r,
):
    gx, core, xi = lax.axis_index("gx"), lax.axis_index("gy"), lax.axis_index("gz")
    zi, yi = gx // 4, lax.rem(gx, 4)
    other = 1 - core
    plane = xi * 4 + yi
    planes = 4 * zn

    def in_plane(d):
        x, y = lax.rem(xi + d // 4, 4), lax.rem(yi + lax.rem(d, 4), 4)
        return x * 4 + y, (zi * 4 + y, core, x)

    def in_column(d):
        z, y = lax.rem(zi + d // 4, zn), lax.rem(yi + lax.rem(d, 4), 4)
        return z * 4 + y, (z * 4 + y, core, xi)

    def load(i):
        return pltpu.make_async_copy(snap.at[:, i], s_buf.at[i], s_sem.at[i])

    load_y = pltpu.make_async_copy(fy, fy_v, f_sem.at[0])
    load_z = pltpu.make_async_copy(fz, fz_v, f_sem.at[1])
    my_fx = fxg.at[rows(yi * 32, 32)]
    load_x = pltpu.make_async_copy(fx, my_fx, f_sem.at[2])
    load_y.start()

    @pl.loop(0, 16)
    def _(i):
        load(i).start()

    load_z.start()
    load_x.start()

    barrier = pltpu.get_barrier_semaphore()
    pl.semaphore_signal(barrier, inc=1, device_id=(gx, other, xi), device_id_type=MESH)

    @pl.loop(1, 16)
    def _(d):
        pl.semaphore_signal(barrier, inc=1, device_id=in_plane(d)[1], device_id_type=MESH)

    @pl.loop(1, zn)
    def _(d):
        pl.semaphore_signal(barrier, inc=1, device_id=in_column(4 * d)[1], device_id_type=MESH)

    load_y.wait()
    ft[...] = fy_v[...].T
    high, low = split(jnp.concatenate([ft[rows(other * 64, 64)], ft[rows(core * 64, 64)]], axis=0))
    fyl[...] = jnp.concatenate([high, low], axis=0)
    load_z.wait()
    fzl[...] = stacked(fz_v[...].T)

    def first_of(i):
        load(i).wait()
        high, low = split(jnp.concatenate([s_buf[i, 0], s_buf[i, 1]], axis=1))
        both = jnp.dot(fyl[...], high, preferred_element_type=F32)
        t = both[:128] + both[128:] + jnp.dot(fyl[0:128], low, preferred_element_type=F32)
        t1s[i, 0:64] = t[:64, :128]
        t1s[i, 64:128] = t[:64, 128:]
        t1o[i, 0:64] = t[64:, :128]
        t1o[i, 64:128] = t[64:, 128:]

    def swap(h):
        part = pl.ds(8 * h, 8)
        return pltpu.make_async_remote_copy(
            src_ref=t1s.at[part], dst_ref=t1r.at[part], send_sem=ys.at[h], recv_sem=yr.at[h],
            device_id=(gx, other, xi), device_id_type=MESH)

    def second_of(h):
        swap(h).wait_recv()

        @pl.loop(0, 4, unroll=UNROLL)
        def _(i):
            at = pl.ds(8 * h + 2 * i, 2)
            t2 = (t1o[at] + t1r[at]).reshape(256, 128)
            w = jnp.concatenate(split(t2), axis=1)
            q = lax.dot_general(fzl[...], w, NT, preferred_element_type=F32)
            q = q[:128] + q[128:]
            t3[h, pl.ds(2 * i, 128, stride=8), :] = q[:, :128]
            t3[h, pl.ds(2 * i + 1, 128, stride=8), :] = q[:, 128:]

    def exchange(h, start, size, sem, d):
        block, to = in_plane(d)
        return pltpu.make_async_remote_copy(
            src_ref=t3.at[h, rows(block * 64 + start, size)], dst_ref=rx.at[h, plane, start:start + size],
            send_sem=x_s.at[sem], recv_sem=x_r.at[sem], device_id=to, device_id_type=MESH)

    def exchange_all(h, start, size, sem):
        @pl.loop(1, 16)
        def _(d):
            exchange(h, start, size, sem, d).start()

    def spread(j, d):
        block, to = in_column(d)
        return pltpu.make_async_remote_copy(
            src_ref=p.at[j, rows(block * 8, 8)], dst_ref=zr.at[j, rows(gx * 8, 8)],
            send_sem=z_s.at[j], recv_sem=z_r.at[j], device_id=to, device_id_type=MESH)

    def gather_fx(d):
        y = lax.rem(yi + d, 4)
        return pltpu.make_async_remote_copy(
            src_ref=my_fx, dst_ref=my_fx, send_sem=g_s, recv_sem=g_r,
            device_id=(zi * 4 + y, core, xi), device_id_type=MESH)

    def wait(ref, sem):
        pltpu.make_async_copy(ref, ref, sem).wait()

    parts = ((0, 0, 64), (1, 0, 32), (1, 32, 32))

    def contract(j):
        add = lambda h: rx[h, 0:4, 32 * j:32 * j + 32] + rx[h, 4:8, 32 * j:32 * j + 32] + (
            rx[h, 8:12, 32 * j:32 * j + 32] + rx[h, 12:16, 32 * j:32 * j + 32])
        sums = [add(0), add(1)]
        turned = [pltpu.roll(s.reshape(128, 128), 64, 1).reshape(4, 32, 128) for s in sums]
        low_half = lax.broadcasted_iota(jnp.int32, (8, 128), 1) < 64
        columns = []
        for q in range(2):
            c0, c1 = slice(8 * q, 8 * q + 8), slice(16 + 8 * q, 24 + 8 * q)
            pieces = []
            for y in range(4):
                for xh in range(2):
                    for h in range(2):
                        if xh == 0:
                            pieces.append(jnp.where(low_half, sums[h][y, c0], turned[h][y, c1]))
                        else:
                            pieces.append(jnp.where(low_half, turned[h][y, c0], sums[h][y, c1]))
            columns.append(jnp.concatenate(pieces, axis=0))
        w = jnp.concatenate(split(jnp.concatenate(columns, axis=1)), axis=0)
        r = jnp.dot(fxl[...], w, preferred_element_type=F32)
        r = r[:128] + r[128:]
        for q in range(2):
            for a in range(4):
                p[j, pl.ds(4 * q + a, planes, stride=8), :] = r[a * planes:(a + 1) * planes, 128 * q:128 * q + 128]

    def total(j):
        w = zr[j, 0:32]
        for z in range(1, zn):
            w = w + zr[j, 32 * z:32 * z + 32]
        turned = pltpu.roll(w, 64, 1)
        for y in range(4):
            at = 32 * y + 16 * j
            fin[at:at + 8] = w[8 * y:8 * y + 8]
            fin[at + 8:at + 16] = turned[8 * y:8 * y + 8]

    @pl.loop(0, 8, unroll=UNROLL)
    def _(i):
        first_of(i)

    load_x.wait()
    pl.semaphore_wait(barrier, 1 + 15 + (zn - 1))
    swap(0).start()

    @pl.loop(1, 4)
    def _(d):
        gather_fx(d).start()

    @pl.loop(8, 16, unroll=UNROLL)
    def _(i):
        first_of(i)

    swap(1).start()
    second_of(0)
    exchange_all(*parts[0], 0)
    second_of(1)
    exchange_all(*parts[1], 1)
    exchange_all(*parts[2], 2)
    for h in range(2):
        rx[h, plane] = t3[h, rows(plane * 64, 64)]
    wait(fxg.at[0:96], g_r)
    fz_v[...] = fxg[...].T
    fxl[...] = stacked(jnp.concatenate([fz_v[pl.ds(a, planes, stride=4), :] for a in range(4)], axis=0))
    wait(rx.at[0, 0:15], x_r.at[0])
    for j in range(CHUNKS):
        wait(rx.at[1, 0:15, 0:32], x_r.at[1 + j])
        contract(j)
        @pl.loop(1, planes)
        def _(d):
            spread(j, d).start()
        zr[j, rows(gx * 8, 8)] = p[j, rows(gx * 8, 8)]
    for j in range(CHUNKS):
        wait(zr.at[j, 0:8 * planes - 8], z_r.at[j])
        total(j)
    for a in range(4):
        out[a] = fin[pl.ds(a, 32, stride=4), :][:, :64]

    for h in range(2):
        swap(h).wait_send()
    wait(fxg.at[0:96], g_s)
    wait(rx.at[0, 0:15], x_s.at[0])
    for j in range(CHUNKS):
        wait(rx.at[1, 0:15, 0:32], x_s.at[1 + j])
    for j in range(CHUNKS):
        wait(zr.at[j, 0:8 * planes - 8], z_s.at[j])


def body(zn, snapshot, factor_x, factor_y, factor_z):
    anywhere = pl.BlockSpec(memory_space=pl.ANY)
    dma = pltpu.SemaphoreType.DMA
    core = pl.pallas_call(
        functools.partial(kernel, zn),
        out_shape=jax.ShapeDtypeStruct((4, 32, 64), F32),
        in_specs=[anywhere] * 4,
        out_specs=pl.BlockSpec(memory_space=pltpu.VMEM),
        scratch_shapes=[
            pltpu.VMEM((16, 2, 256, 128), F32),
            pltpu.VMEM((256, 128), F32),
            pltpu.VMEM((128, 128), F32),
            pltpu.VMEM((128, 128), F32),
            pltpu.VMEM((128, 256), F32),
            pltpu.VMEM((256, 256), BF16),
            pltpu.VMEM((256, 256), BF16),
            pltpu.VMEM((256, 256), BF16),
            pltpu.VMEM((16, 128, 128), F32),
            pltpu.VMEM((16, 128, 128), F32),
            pltpu.VMEM((16, 128, 128), F32),
            pltpu.VMEM((2, 1024, 128), F32),
            pltpu.VMEM((2, 16, 64, 128), F32),
            pltpu.VMEM((CHUNKS, 32 * zn, 128), F32),
            pltpu.VMEM((CHUNKS, 32 * zn, 128), F32),
            pltpu.VMEM((128, 128), F32),
            dma((16,)), dma((3,)), dma((2,)), dma((2,)),
            dma((3,)), dma((3,)), dma((CHUNKS,)), dma((CHUNKS,)), dma, dma,
        ],
        compiler_params=pltpu.CompilerParams(
            collective_id=0, has_side_effects=True, vmem_limit_bytes=64 * 1024 * 1024
        ),
    )(snapshot.reshape(2, 16, 256, 128), factor_x, factor_y, factor_z)
    return core.transpose(0, 2, 1)


def solution(mesh):
    return jax.shard_map(
        functools.partial(body, mesh.shape["gx"] // 4),
        mesh=mesh,
        in_specs=(P("gx", "gy", "gz"), P("gx", None), P("gy", None), P("gz", None)),
        out_specs=P("gx", "gy", "gz"),
        check_vma=False,
    )
```

```python
import functools

import jax
import jax.numpy as jnp
from jax import lax
from jax.experimental import pallas as pl
from jax.experimental.pallas import tpu as pltpu
from jax.sharding import PartitionSpec as P

MESH = pl.DeviceIdType.MESH
F32, BF16 = jnp.float32, jnp.bfloat16
NT = (((1,), (1,)), ((), ()))
CHUNKS = 2


def split(value):
    high = value.astype(BF16)
    return high, (value - high.astype(F32)).astype(BF16)


def rows(start, size):
    return pl.ds(pl.multiple_of(start, 8), size)


def stacked(factor_t):
    high, low = split(factor_t)
    top = jnp.concatenate([high, high], axis=1)
    return jnp.concatenate([top, jnp.concatenate([low, jnp.zeros_like(low)], axis=1)], axis=0)


def kernel(
    zn, snap, fx, fy, fz, out,
    s_buf, fy_v, fz_v, fxg, ft, fyl, fzl, fxl, t1s, t1o, t1r, t3, rx, rx1, p, zr, fin,
    s_sem, f_sem, ys, yr, r_s, r_r, x_s, x_r, z_s, z_r, g_s, g_r,
):
    gx, core, xi = lax.axis_index("gx"), lax.axis_index("gy"), lax.axis_index("gz")
    zi, yi = gx // 4, lax.rem(gx, 4)
    other = 1 - core
    plane = xi * 4 + yi
    planes = 4 * zn

    right, opposite, left = lax.rem(xi + 1, 4), lax.rem(xi + 2, 4), lax.rem(xi + 3, 4)

    def in_plane(d):
        x, y = lax.rem(xi + d // 4, 4), lax.rem(yi + lax.rem(d, 4), 4)
        return (zi * 4 + y, core, x)

    def in_column(d):
        z, y = lax.rem(zi + d // 4, zn), lax.rem(yi + lax.rem(d, 4), 4)
        return z * 4 + y, (z * 4 + y, core, xi)

    def load(i):
        return pltpu.make_async_copy(snap.at[:, i], s_buf.at[i], s_sem.at[i])

    load_y = pltpu.make_async_copy(fy, fy_v, f_sem.at[0])
    load_z = pltpu.make_async_copy(fz, fz_v, f_sem.at[1])
    my_fx = fxg.at[rows(yi * 32, 32)]
    load_x = pltpu.make_async_copy(fx, my_fx, f_sem.at[2])
    load_y.start()

    @pl.loop(0, 16)
    def _(i):
        load(i).start()

    load_z.start()
    load_x.start()

    barrier = pltpu.get_barrier_semaphore()
    pl.semaphore_signal(barrier, inc=1, device_id=(gx, other, xi), device_id_type=MESH)

    @pl.loop(1, 16)
    def _(d):
        pl.semaphore_signal(barrier, inc=1, device_id=in_plane(d), device_id_type=MESH)

    @pl.loop(1, zn)
    def _(d):
        pl.semaphore_signal(barrier, inc=1, device_id=in_column(4 * d)[1], device_id_type=MESH)

    load_y.wait()
    ft[...] = fy_v[...].T
    high, low = split(jnp.concatenate([ft[rows(other * 64, 64)], ft[rows(core * 64, 64)]], axis=0))
    fyl[...] = jnp.concatenate([high, low], axis=0)
    load_z.wait()
    fzl[...] = stacked(fz_v[...].T)

    def first_of(i):
        load(i).wait()
        high, low = split(jnp.concatenate([s_buf[i, 0], s_buf[i, 1]], axis=1))
        both = jnp.dot(fyl[...], high, preferred_element_type=F32)
        t = both[:128] + both[128:] + jnp.dot(fyl[0:128], low, preferred_element_type=F32)
        t1s[i, 0:64] = t[:64, :128]
        t1s[i, 64:128] = t[:64, 128:]
        t1o[i, 0:64] = t[64:, :128]
        t1o[i, 64:128] = t[64:, 128:]

    def swap(h):
        part = pl.ds(8 * h, 8)
        return pltpu.make_async_remote_copy(
            src_ref=t1s.at[part], dst_ref=t1r.at[part], send_sem=ys.at[h], recv_sem=yr.at[h],
            device_id=(gx, other, xi), device_id_type=MESH)

    def second_of(h):
        swap(h).wait_recv()

        @pl.loop(0, 4)
        def _(i):
            at = pl.ds(8 * h + 2 * i, 2)
            t2 = (t1o[at] + t1r[at]).reshape(256, 128)
            w = jnp.concatenate(split(t2), axis=1)
            q = lax.dot_general(fzl[...], w, NT, preferred_element_type=F32)
            q = q[:128] + q[128:]
            t3[h, pl.ds(2 * i, 128, stride=8), :] = q[:, :128]
            t3[h, pl.ds(2 * i + 1, 128, stride=8), :] = q[:, 128:]

    def relay(h, way):
        return pltpu.make_async_remote_copy(
            src_ref=t3.at[h, rows(opposite * 256 + way * 128, 128)], dst_ref=rx1.at[way, h],
            send_sem=r_s.at[way, h], recv_sem=r_r.at[way, h],
            device_id=(gx, core, (right, left)[way]), device_id_type=MESH)

    def exchange(part, x, y, slot):
        h, start, size, sem = part
        pltpu.make_async_remote_copy(
            src_ref=t3.at[h, rows(x * 256 + y * 64 + start, size)],
            dst_ref=rx.at[h, slot * 4 + yi, start:start + size],
            send_sem=x_s.at[sem], recv_sem=x_r.at[sem],
            device_id=(zi * 4 + y, core, x), device_id_type=MESH).start()

    def send_plain(part):
        @pl.loop(1, 4)
        def _(d):
            exchange(part, xi, lax.rem(yi + d, 4), 1)

        @pl.loop(0, 2)
        def _(y):
            exchange(part, right, y + 2, 0)
            exchange(part, left, y, 2)

    def merge(h):
        for way in range(2):
            relay(h, way).wait_recv()
            at = rows((right, left)[way] * 256 + way * 128, 128)
            t3[h, at] = t3[h, at] + rx1[way, h]

    def send_merged(part):
        @pl.loop(0, 2)
        def _(y):
            exchange(part, right, y, 0)
            exchange(part, left, y + 2, 2)

    def spread(j, d):
        block, to = in_column(d)
        return pltpu.make_async_remote_copy(
            src_ref=p.at[j, rows(block * 8, 8)], dst_ref=zr.at[j, rows(gx * 8, 8)],
            send_sem=z_s.at[j], recv_sem=z_r.at[j], device_id=to, device_id_type=MESH)

    def gather_fx(d):
        y = lax.rem(yi + d, 4)
        return pltpu.make_async_remote_copy(
            src_ref=my_fx, dst_ref=my_fx, send_sem=g_s, recv_sem=g_r,
            device_id=(zi * 4 + y, core, xi), device_id_type=MESH)

    def wait(ref, sem):
        pltpu.make_async_copy(ref, ref, sem).wait()

    parts = ((0, 0, 64, 0), (1, 0, 32, 1), (1, 32, 32, 2))

    def contract(j):
        at = slice(32 * j, 32 * j + 32)
        add = lambda h: rx[h, 0:4, at] + rx[h, 4:8, at] + rx[h, 8:12, at]
        sums = [add(0), add(1)]
        turned = [pltpu.roll(s.reshape(128, 128), 64, 1).reshape(4, 32, 128) for s in sums]
        low_half = lax.broadcasted_iota(jnp.int32, (8, 128), 1) < 64
        columns = []
        for q in range(2):
            c0, c1 = slice(8 * q, 8 * q + 8), slice(16 + 8 * q, 24 + 8 * q)
            pieces = []
            for y in range(4):
                for xh in range(2):
                    for h in range(2):
                        if xh == 0:
                            pieces.append(jnp.where(low_half, sums[h][y, c0], turned[h][y, c1]))
                        else:
                            pieces.append(jnp.where(low_half, turned[h][y, c0], sums[h][y, c1]))
            columns.append(jnp.concatenate(pieces, axis=0))
        w = jnp.concatenate(split(jnp.concatenate(columns, axis=1)), axis=0)
        r = jnp.dot(fxl[...], w, preferred_element_type=F32)
        r = r[:128] + r[128:]
        for q in range(2):
            for a in range(4):
                p[j, pl.ds(4 * q + a, planes, stride=8), :] = r[a * planes:(a + 1) * planes, 128 * q:128 * q + 128]

    def total(j):
        w = zr[j, 0:32]
        for z in range(1, zn):
            w = w + zr[j, 32 * z:32 * z + 32]
        turned = pltpu.roll(w, 64, 1)
        for y in range(4):
            at = 32 * y + 16 * j
            fin[at:at + 8] = w[8 * y:8 * y + 8]
            fin[at + 8:at + 16] = turned[8 * y:8 * y + 8]

    @pl.loop(0, 8)
    def _(i):
        first_of(i)

    load_x.wait()
    pl.semaphore_wait(barrier, 1 + 15 + (zn - 1))
    swap(0).start()

    @pl.loop(1, 4)
    def _(d):
        gather_fx(d).start()

    @pl.loop(8, 16)
    def _(i):
        first_of(i)

    swap(1).start()
    second_of(0)
    for way in range(2):
        relay(0, way).start()
    send_plain(parts[0])
    second_of(1)
    for way in range(2):
        relay(1, way).start()
    send_plain(parts[1])
    merge(0)
    send_merged(parts[0])
    send_plain(parts[2])
    merge(1)
    send_merged(parts[1])
    send_merged(parts[2])
    for h in range(2):
        rx[h, 4 + yi] = t3[h, rows(plane * 64, 64)]
    wait(fxg.at[0:96], g_r)
    fz_v[...] = fxg[...].T
    fxl[...] = stacked(jnp.concatenate([fz_v[pl.ds(a, planes, stride=4), :] for a in range(4)], axis=0))
    wait(rx.at[0, 0:11], x_r.at[0])
    for j in range(CHUNKS):
        wait(rx.at[1, 0:11, 0:32], x_r.at[1 + j])
        contract(j)
        @pl.loop(1, planes)
        def _(d):
            spread(j, d).start()
        zr[j, rows(gx * 8, 8)] = p[j, rows(gx * 8, 8)]
    for j in range(CHUNKS):
        wait(zr.at[j, 0:8 * planes - 8], z_r.at[j])
        total(j)
    for a in range(4):
        out[a] = fin[pl.ds(a, 32, stride=4), :][:, :64]

    for h in range(2):
        swap(h).wait_send()
    wait(fxg.at[0:96], g_s)
    wait(rx.at[0, 0:11], x_s.at[0])
    for j in range(CHUNKS):
        wait(rx.at[1, 0:11, 0:32], x_s.at[1 + j])
    for h in range(2):
        for way in range(2):
            relay(h, way).wait_send()
    for j in range(CHUNKS):
        wait(zr.at[j, 0:8 * planes - 8], z_s.at[j])


def body(zn, snapshot, factor_x, factor_y, factor_z):
    anywhere = pl.BlockSpec(memory_space=pl.ANY)
    dma = pltpu.SemaphoreType.DMA
    core = pl.pallas_call(
        functools.partial(kernel, zn),
        out_shape=jax.ShapeDtypeStruct((4, 32, 64), F32),
        in_specs=[anywhere] * 4,
        out_specs=pl.BlockSpec(memory_space=pltpu.VMEM),
        scratch_shapes=[
            pltpu.VMEM((16, 2, 256, 128), F32),
            pltpu.VMEM((256, 128), F32),
            pltpu.VMEM((128, 128), F32),
            pltpu.VMEM((128, 128), F32),
            pltpu.VMEM((128, 256), F32),
            pltpu.VMEM((256, 256), BF16),
            pltpu.VMEM((256, 256), BF16),
            pltpu.VMEM((256, 256), BF16),
            pltpu.VMEM((16, 128, 128), F32),
            pltpu.VMEM((16, 128, 128), F32),
            pltpu.VMEM((16, 128, 128), F32),
            pltpu.VMEM((2, 1024, 128), F32),
            pltpu.VMEM((2, 12, 64, 128), F32),
            pltpu.VMEM((2, 2, 128, 128), F32),
            pltpu.VMEM((CHUNKS, 32 * zn, 128), F32),
            pltpu.VMEM((CHUNKS, 32 * zn, 128), F32),
            pltpu.VMEM((128, 128), F32),
            dma((16,)), dma((3,)), dma((2,)), dma((2,)),
            dma((2, 2)), dma((2, 2)), dma((3,)), dma((3,)), dma((CHUNKS,)), dma((CHUNKS,)), dma, dma,
        ],
        compiler_params=pltpu.CompilerParams(
            collective_id=0, has_side_effects=True, vmem_limit_bytes=64 * 1024 * 1024
        ),
    )(snapshot.reshape(2, 16, 256, 128), factor_x, factor_y, factor_z)
    return core.transpose(0, 2, 1)


def solution(mesh):
    return jax.shard_map(
        functools.partial(body, mesh.shape["gx"] // 4),
        mesh=mesh,
        in_specs=(P("gx", "gy", "gz"), P("gx", None), P("gy", None), P("gz", None)),
        out_specs=P("gx", "gy", "gz"),
        check_vma=False,
    )
```

```python
import functools

import jax
import jax.numpy as jnp
from jax import lax
from jax.experimental import pallas as pl
from jax.experimental.pallas import tpu as pltpu
from jax.sharding import PartitionSpec as P

MESH = pl.DeviceIdType.MESH
F32, BF16 = jnp.float32, jnp.bfloat16
NT = (((1,), (1,)), ((), ()))
CHUNKS = 2
WIDTH = 8 // CHUNKS
PAIRS = WIDTH // 2


def split(value):
    high = value.astype(BF16)
    return high, (value - high.astype(F32)).astype(BF16)


def rows(start, size):
    return pl.ds(pl.multiple_of(start, 8), size)


def stacked(factor_t):
    high, low = split(factor_t)
    top = jnp.concatenate([high, high], axis=1)
    return jnp.concatenate([top, jnp.concatenate([low, jnp.zeros_like(low)], axis=1)], axis=0)


def kernel(
    zn, snap, fx, fy, fz, out,
    s_buf, fy_v, fz_v, fxg, ft, fyl, fzl, fxl, t1s, t1o, t1r, t3, rx, rx1, p, zr, fin,
    s_sem, f_sem, ys, yr, r_s, r_r, x_s, x_r, z_s, z_r, g_s, g_r,
):
    gx, core, xi = lax.axis_index("gx"), lax.axis_index("gy"), lax.axis_index("gz")
    zi, yi = gx // 4, lax.rem(gx, 4)
    other = 1 - core
    plane = xi * 4 + yi
    planes = 4 * zn

    right, opposite, left = lax.rem(xi + 1, 4), lax.rem(xi + 2, 4), lax.rem(xi + 3, 4)

    def in_plane(d):
        x, y = lax.rem(xi + d // 4, 4), lax.rem(yi + lax.rem(d, 4), 4)
        return (zi * 4 + y, core, x)

    def in_column(d):
        z, y = lax.rem(zi + d // 4, zn), lax.rem(yi + lax.rem(d, 4), 4)
        return z * 4 + y, (z * 4 + y, core, xi)

    def load(i):
        return pltpu.make_async_copy(snap.at[:, i], s_buf.at[i], s_sem.at[i])

    load_y = pltpu.make_async_copy(fy, fy_v, f_sem.at[0])
    load_z = pltpu.make_async_copy(fz, fz_v, f_sem.at[1])
    my_fx = fxg.at[rows(yi * 32, 32)]
    load_x = pltpu.make_async_copy(fx, my_fx, f_sem.at[2])
    load_y.start()

    @pl.loop(0, 16)
    def _(i):
        load(i).start()

    load_z.start()
    load_x.start()

    barrier = pltpu.get_barrier_semaphore()
    pl.semaphore_signal(barrier, inc=1, device_id=(gx, other, xi), device_id_type=MESH)

    @pl.loop(1, 16)
    def _(d):
        pl.semaphore_signal(barrier, inc=1, device_id=in_plane(d), device_id_type=MESH)

    @pl.loop(1, zn)
    def _(d):
        pl.semaphore_signal(barrier, inc=1, device_id=in_column(4 * d)[1], device_id_type=MESH)

    load_y.wait()
    ft[...] = fy_v[...].T
    high, low = split(jnp.concatenate([ft[rows(other * 64, 64)], ft[rows(core * 64, 64)]], axis=0))
    fyl[...] = jnp.concatenate([high, low], axis=0)
    load_z.wait()
    group = 4 * WIDTH
    fz_t = fz_v[...].T
    fzl[...] = stacked(jnp.concatenate(
        [fz_t[32 * x + group * j:32 * x + group * (j + 1)] for j in range(CHUNKS) for x in range(4)], axis=0))

    def first_of(i):
        load(i).wait()
        high, low = split(jnp.concatenate([s_buf[i, 0], s_buf[i, 1]], axis=1))
        both = jnp.dot(fyl[...], high, preferred_element_type=F32)
        t = both[:128] + both[128:] + jnp.dot(fyl[0:128], low, preferred_element_type=F32)
        t1s[i, 0:64] = t[:64, :128]
        t1s[i, 64:128] = t[:64, 128:]
        t1o[i, 0:64] = t[64:, :128]
        t1o[i, 64:128] = t[64:, 128:]

    def swap(part):
        at = pl.ds(4 * part, 4)
        return pltpu.make_async_remote_copy(
            src_ref=t1s.at[at], dst_ref=t1r.at[at], send_sem=ys.at[part], recv_sem=yr.at[part],
            device_id=(gx, other, xi), device_id_type=MESH)

    def second_of(part):
        swap(part).wait_recv()
        for i in range(2):
            n = 4 * part + 2 * i
            t2 = (t1o[n:n + 2] + t1r[n:n + 2]).reshape(256, 128)
            w = jnp.concatenate(split(t2), axis=1)
            q = lax.dot_general(fzl[...], w, NT, preferred_element_type=F32)
            q = q[:128] + q[128:]
            t3[pl.ds(n, 128, stride=16), :] = q[:, :128]
            t3[pl.ds(n + 1, 128, stride=16), :] = q[:, 128:]

    def block_of(part, x, y, number):
        j, h = part[:2]
        at = ((j * 4 + x) * 4 + y) * WIDTH
        if h is None:
            return t3.at[pl.ds(pl.multiple_of(at * 16, 32), number * 16)]
        return t3.reshape(128, 2, 8, 128).at[pl.ds(at, number), h]

    def slot_of(ref, part, at):
        j, h = part[:2]
        if h is None:
            return ref.at[j, at]
        return ref.reshape(*ref.shape[:-2], ref.shape[-2] // 16, 2, 8, 128).at[j, at, :, h]

    def relay(part, way):
        return pltpu.make_async_remote_copy(
            src_ref=block_of(part, opposite, 2 * way, 2 * WIDTH), dst_ref=slot_of(rx1, part, way),
            send_sem=r_s.at[part[2], way], recv_sem=r_r.at[part[2], way],
            device_id=(gx, core, (right, left)[way]), device_id_type=MESH)

    def send_relay(part):
        for way in range(2):
            relay(part, way).start()

    def exchange(part, x, y, slot):
        pltpu.make_async_remote_copy(
            src_ref=block_of(part, x, y, WIDTH), dst_ref=slot_of(rx, part, slot * 4 + yi),
            send_sem=x_s.at[part[2]], recv_sem=x_r.at[part[2]],
            device_id=(zi * 4 + y, core, x), device_id_type=MESH).start()

    def send_plain(part):
        @pl.loop(1, 4)
        def _(d):
            exchange(part, xi, lax.rem(yi + d, 4), 1)

        @pl.loop(0, 2)
        def _(y):
            exchange(part, right, y + 2, 0)
            exchange(part, left, y, 2)

    def send_merged(part):
        for way in range(2):
            relay(part, way).wait_recv()
            to = block_of(part, (right, left)[way], 2 * way, 2 * WIDTH)
            to[...] = to[...] + slot_of(rx1, part, way)[...]

        @pl.loop(0, 2)
        def _(y):
            exchange(part, right, y, 0)
            exchange(part, left, y + 2, 2)

    def spread(j, d):
        block, to = in_column(d)
        return pltpu.make_async_remote_copy(
            src_ref=p.at[j, block], dst_ref=zr.at[j, gx],
            send_sem=z_s.at[j], recv_sem=z_r.at[j], device_id=to, device_id_type=MESH)

    def gather_fx(d):
        y = lax.rem(yi + d, 4)
        return pltpu.make_async_remote_copy(
            src_ref=my_fx, dst_ref=my_fx, send_sem=g_s, recv_sem=g_r,
            device_id=(zi * 4 + y, core, xi), device_id_type=MESH)

    dummy = t3

    def wait(ref, sem):
        pltpu.make_async_copy(ref, ref, sem).wait()

    parts = [(0, 0, 0), (0, 1, 1)] + [(j, None, 1 + j) for j in range(1, CHUNKS)]

    def contract(j):
        add = rx[j, 0:4] + rx[j, 4:8] + rx[j, 8:12]
        turned = pltpu.roll(add.reshape(-1, 128), 64, 1).reshape(add.shape)
        low_half = lax.broadcasted_iota(jnp.int32, (16, 128), 1) < 64
        columns = []
        for q in range(PAIRS):
            c0, c1 = slice(16 * q, 16 * q + 16), slice(16 * (PAIRS + q), 16 * (PAIRS + q) + 16)
            pieces = []
            for y in range(4):
                pieces.append(jnp.where(low_half, add[y, c0], turned[y, c1]))
                pieces.append(jnp.where(low_half, turned[y, c0], add[y, c1]))
            columns.append(jnp.concatenate(pieces, axis=0))
        w = jnp.concatenate(split(jnp.concatenate(columns, axis=1)), axis=0)
        r = jnp.dot(fxl[...], w, preferred_element_type=F32)
        r = r[:128] + r[128:]
        for q in range(PAIRS):
            p[j, :, 4 * q:4 * q + 4] = r[:, 128 * q:128 * q + 128].reshape(planes, 4, 128)

    def total(j):
        w = zr[j, 0:4]
        for z in range(1, zn):
            w = w + zr[j, 4 * z:4 * z + 4]
        for y in range(4):
            turned = pltpu.roll(w[y], 64, 1)
            at = (j * 4 + y) * WIDTH * 4
            fin[at:at + 4 * PAIRS] = w[y]
            fin[at + 4 * PAIRS:at + 8 * PAIRS] = turned

    def do_spread(j):
        contract(j)

        @pl.loop(0, planes - 1)
        def _(i):
            k = i // 4
            z = lax.rem(zn // 2 + (k + 1) // 2 * (1 - 2 * lax.rem(k, 2)) + zn, zn)
            spread(j, 4 * z + 3 - lax.rem(i, 4)).start()

        zr[j, gx] = p[j, gx]

    def await_part(n):
        size = slice(0, 11 * WIDTH * 16 // (2 if n < 2 else 1))
        wait(dummy.at[size], x_r.at[n])

    def first(part):
        @pl.loop(4 * part, 4 * part + 4)
        def _(i):
            first_of(i)

    entered = lambda: pl.semaphore_wait(barrier, 1 + 15 + (zn - 1))
    for part in range(4):
        first(part)
        if part == 1:
            load_x.wait()
            entered()
            for n in range(part):
                swap(n).start()
        if part >= 1:
            swap(part).start()
        if part == 1:
            @pl.loop(1, 4)
            def _(d):
                gather_fx(d).start()
        if part == 2:
            second_of(0)
            second_of(1)
            send_relay(parts[0])
            send_plain(parts[0])
    second_of(2)
    second_of(3)
    send_relay(parts[1])
    send_plain(parts[1])
    rx[0, 4 + yi] = t3[rows(plane * WIDTH * 16, WIDTH * 16)]
    for j in range(1, CHUNKS):
        rx[j, 4 + yi] = t3[rows((j * 16 + plane) * WIDTH * 16, WIDTH * 16)]
    send_relay(parts[2])
    send_merged(parts[0])
    wait(fxg.at[0:96], g_r)
    fxl[...] = stacked(fxg[...].T)
    send_merged(parts[1])
    for j in range(1, CHUNKS):
        send_plain(parts[1 + j])
        if j + 1 < CHUNKS:
            send_relay(parts[2 + j])
        send_merged(parts[1 + j])
    for j in range(CHUNKS):
        if j == 0:
            await_part(0)
            await_part(1)
        else:
            await_part(j + 1)
        do_spread(j)
    for j in range(CHUNKS):
        wait(zr.at[j, 0:planes - 1], z_r.at[j])
        total(j)
    for a in range(4):
        out[a] = fin[pl.ds(a, 32, stride=4), :][:, :64]

    for n in range(4):
        swap(n).wait_send()
    wait(fxg.at[0:96], g_s)
    for n, part in enumerate(parts):
        for way in range(2):
            relay(part, way).wait_send()
        wait(dummy.at[0:11 * WIDTH * 16 // (2 if n < 2 else 1)], x_s.at[n])
    for j in range(CHUNKS):
        wait(zr.at[j, 0:planes - 1], z_s.at[j])


def body(zn, snapshot, factor_x, factor_y, factor_z):
    anywhere = pl.BlockSpec(memory_space=pl.ANY)
    dma = pltpu.SemaphoreType.DMA
    core = pl.pallas_call(
        functools.partial(kernel, zn),
        out_shape=jax.ShapeDtypeStruct((4, 32, 64), F32),
        in_specs=[anywhere] * 4,
        out_specs=pl.BlockSpec(memory_space=pltpu.VMEM),
        scratch_shapes=[
            pltpu.VMEM((16, 2, 256, 128), F32),
            pltpu.VMEM((256, 128), F32),
            pltpu.VMEM((128, 128), F32),
            pltpu.VMEM((128, 128), F32),
            pltpu.VMEM((128, 256), F32),
            pltpu.VMEM((256, 256), BF16),
            pltpu.VMEM((256, 256), BF16),
            pltpu.VMEM((256, 256), BF16),
            pltpu.VMEM((16, 128, 128), F32),
            pltpu.VMEM((16, 128, 128), F32),
            pltpu.VMEM((16, 128, 128), F32),
            pltpu.VMEM((2048, 128), F32),
            pltpu.VMEM((CHUNKS, 12, WIDTH * 16, 128), F32),
            pltpu.VMEM((CHUNKS, 2, WIDTH * 32, 128), F32),
            pltpu.VMEM((CHUNKS, 4 * zn, 4 * PAIRS, 128), F32),
            pltpu.VMEM((CHUNKS, 4 * zn, 4 * PAIRS, 128), F32),
            pltpu.VMEM((128, 128), F32),
            dma((16,)), dma((3,)), dma((4,)), dma((4,)),
            dma((1 + CHUNKS, 2)), dma((1 + CHUNKS, 2)), dma((1 + CHUNKS,)), dma((1 + CHUNKS,)), dma((CHUNKS,)), dma((CHUNKS,)), dma, dma,
        ],
        compiler_params=pltpu.CompilerParams(
            collective_id=0, has_side_effects=True, vmem_limit_bytes=64 * 1024 * 1024
        ),
    )(snapshot.reshape(2, 16, 256, 128), factor_x, factor_y, factor_z)
    return core.transpose(0, 2, 1)


def solution(mesh):
    return jax.shard_map(
        functools.partial(body, mesh.shape["gx"] // 4),
        mesh=mesh,
        in_specs=(P("gx", "gy", "gz"), P("gx", None), P("gy", None), P("gz", None)),
        out_specs=P("gx", "gy", "gz"),
        check_vma=False,
    )
```

```python
import functools

import jax
import jax.numpy as jnp
from jax import lax
from jax.experimental import pallas as pl
from jax.experimental.pallas import tpu as pltpu
from jax.sharding import PartitionSpec as P

MESH = pl.DeviceIdType.MESH
F32, BF16 = jnp.float32, jnp.bfloat16
NT = (((1,), (1,)), ((), ()))
CHUNKS = 2
WIDTH = 8 // CHUNKS
PAIRS = WIDTH // 2


def split(value):
    high = value.astype(BF16)
    return high, (value - high.astype(F32)).astype(BF16)


def rows(start, size):
    return pl.ds(pl.multiple_of(start, 8), size)


def stacked(factor_t):
    high, low = split(factor_t)
    top = jnp.concatenate([high, high], axis=1)
    return jnp.concatenate([top, jnp.concatenate([low, jnp.zeros_like(low)], axis=1)], axis=0)


def kernel(
    zn, snap, fx, fy, fz, out,
    s_buf, fy_v, fz_v, fxg, ft, fyl, fzl, fxl, t1s, t1o, t1r, t3, rx, rx1, p, zr, fin,
    s_sem, f_sem, ys, yr, r_s, r_r, x_s, x_r, z_s, z_r, g_s, g_r,
):
    gx, core, xi = lax.axis_index("gx"), lax.axis_index("gy"), lax.axis_index("gz")
    zi, yi = gx // 4, lax.rem(gx, 4)
    other = 1 - core
    plane = xi * 4 + yi
    planes = 4 * zn

    right, opposite, left = lax.rem(xi + 1, 4), lax.rem(xi + 2, 4), lax.rem(xi + 3, 4)

    def in_plane(d):
        x, y = lax.rem(xi + d // 4, 4), lax.rem(yi + lax.rem(d, 4), 4)
        return (zi * 4 + y, core, x)

    def in_column(d):
        z, y = lax.rem(zi + d // 4, zn), lax.rem(yi + lax.rem(d, 4), 4)
        return z * 4 + y, (z * 4 + y, core, xi)

    def load(i):
        return pltpu.make_async_copy(snap.at[:, i], s_buf.at[i], s_sem.at[i])

    load_y = pltpu.make_async_copy(fy, fy_v, f_sem.at[0])
    load_z = pltpu.make_async_copy(fz, fz_v, f_sem.at[1])
    my_fx = fxg.at[rows(yi * 32, 32)]
    load_x = pltpu.make_async_copy(fx, my_fx, f_sem.at[2])
    load_y.start()

    @pl.loop(0, 16)
    def _(i):
        load(i).start()

    load_z.start()
    load_x.start()

    barrier = pltpu.get_barrier_semaphore()
    pl.semaphore_signal(barrier, inc=1, device_id=(gx, other, xi), device_id_type=MESH)

    @pl.loop(1, 16)
    def _(d):
        pl.semaphore_signal(barrier, inc=1, device_id=in_plane(d), device_id_type=MESH)

    @pl.loop(1, zn)
    def _(d):
        pl.semaphore_signal(barrier, inc=1, device_id=in_column(4 * d)[1], device_id_type=MESH)

    load_y.wait()
    ft[...] = fy_v[...].T
    high, low = split(jnp.concatenate([ft[rows(other * 64, 64)], ft[rows(core * 64, 64)]], axis=0))
    fyl[...] = jnp.concatenate([high, low], axis=0)
    load_z.wait()
    group = 4 * WIDTH
    fz_t = fz_v[...].T
    fzl[...] = stacked(jnp.concatenate(
        [fz_t[32 * x + group * j:32 * x + group * (j + 1)] for j in range(CHUNKS) for x in range(4)], axis=0))

    def first_of(i):
        load(i).wait()
        high, low = split(jnp.concatenate([s_buf[i, 0], s_buf[i, 1]], axis=1))
        both = jnp.dot(fyl[...], high, preferred_element_type=F32)
        t = both[:128] + both[128:] + jnp.dot(fyl[0:128], low, preferred_element_type=F32)
        t1s[i, 0:64] = t[:64, :128]
        t1s[i, 64:128] = t[:64, 128:]
        t1o[i, 0:64] = t[64:, :128]
        t1o[i, 64:128] = t[64:, 128:]

    def swap(part):
        at = pl.ds(4 * part, 4)
        return pltpu.make_async_remote_copy(
            src_ref=t1s.at[at], dst_ref=t1r.at[at], send_sem=ys.at[part], recv_sem=yr.at[part],
            device_id=(gx, other, xi), device_id_type=MESH)

    def second_of(part):
        swap(part).wait_recv()
        for i in range(2):
            n = 4 * part + 2 * i
            t2 = (t1o[n:n + 2] + t1r[n:n + 2]).reshape(256, 128)
            w = jnp.concatenate(split(t2), axis=1)
            q = lax.dot_general(fzl[...], w, NT, preferred_element_type=F32)
            q = q[:128] + q[128:]
            t3[pl.ds(n, 128, stride=16), :] = q[:, :128]
            t3[pl.ds(n + 1, 128, stride=16), :] = q[:, 128:]

    def block_of(part, x, y, number):
        j, h = part[:2]
        at = ((j * 4 + x) * 4 + y) * WIDTH
        if h is None:
            return t3.at[pl.ds(pl.multiple_of(at * 16, 32), number * 16)]
        return t3.reshape(128, 2, 8, 128).at[pl.ds(at, number), h]

    def slot_of(ref, part, at):
        j, h = part[:2]
        if h is None:
            return ref.at[j, at]
        return ref.reshape(*ref.shape[:-2], ref.shape[-2] // 16, 2, 8, 128).at[j, at, :, h]

    def relay(part, way):
        return pltpu.make_async_remote_copy(
            src_ref=block_of(part, opposite, 2 * way, 2 * WIDTH), dst_ref=slot_of(rx1, part, way),
            send_sem=r_s.at[part[2], way], recv_sem=r_r.at[part[2], way],
            device_id=(gx, core, (right, left)[way]), device_id_type=MESH)

    def send_relay(part):
        for way in range(2):
            relay(part, way).start()

    def exchange(part, x, y, slot):
        pltpu.make_async_remote_copy(
            src_ref=block_of(part, x, y, WIDTH), dst_ref=slot_of(rx, part, slot * 4 + yi),
            send_sem=x_s.at[part[2]], recv_sem=x_r.at[part[2]],
            device_id=(zi * 4 + y, core, x), device_id_type=MESH).start()

    def send_plain(part):
        @pl.loop(1, 4)
        def _(d):
            exchange(part, xi, lax.rem(yi + d, 4), 1)

        @pl.loop(0, 2)
        def _(y):
            exchange(part, right, y + 2, 0)
            exchange(part, left, y, 2)

    def send_merged(part):
        for way in range(2):
            relay(part, way).wait_recv()
            to = block_of(part, (right, left)[way], 2 * way, 2 * WIDTH)
            to[...] = to[...] + slot_of(rx1, part, way)[...]

        @pl.loop(0, 2)
        def _(y):
            exchange(part, right, y, 0)
            exchange(part, left, y + 2, 2)

    def spread(j, d):
        block, to = in_column(d)
        return pltpu.make_async_remote_copy(
            src_ref=p.at[j, block], dst_ref=zr.at[j, gx],
            send_sem=z_s.at[j], recv_sem=z_r.at[j], device_id=to, device_id_type=MESH)

    def gather_fx(d):
        y = lax.rem(yi + d, 4)
        return pltpu.make_async_remote_copy(
            src_ref=my_fx, dst_ref=my_fx, send_sem=g_s, recv_sem=g_r,
            device_id=(zi * 4 + y, core, xi), device_id_type=MESH)

    dummy = t3

    def wait(ref, sem):
        pltpu.make_async_copy(ref, ref, sem).wait()

    parts = [(0, 0, 0), (0, 1, 1)] + [(j, None, 1 + j) for j in range(1, CHUNKS)]

    def contract(j):
        add = rx[j, 0:4] + rx[j, 4:8] + rx[j, 8:12]
        turned = pltpu.roll(add.reshape(-1, 128), 64, 1).reshape(add.shape)
        low_half = lax.broadcasted_iota(jnp.int32, (16, 128), 1) < 64
        columns = []
        for q in range(PAIRS):
            c0, c1 = slice(16 * q, 16 * q + 16), slice(16 * (PAIRS + q), 16 * (PAIRS + q) + 16)
            pieces = []
            for y in range(4):
                pieces.append(jnp.where(low_half, add[y, c0], turned[y, c1]))
                pieces.append(jnp.where(low_half, turned[y, c0], add[y, c1]))
            columns.append(jnp.concatenate(pieces, axis=0))
        w = jnp.concatenate(split(jnp.concatenate(columns, axis=1)), axis=0)
        r = jnp.dot(fxl[...], w, preferred_element_type=F32)
        r = r[:128] + r[128:]
        for q in range(PAIRS):
            p[j, :, 4 * q:4 * q + 4] = r[:, 128 * q:128 * q + 128].reshape(planes, 4, 128)

    def total(j):
        w = zr[j, 0:4]
        for z in range(1, zn):
            w = w + zr[j, 4 * z:4 * z + 4]
        for y in range(4):
            turned = pltpu.roll(w[y], 64, 1)
            at = (j * 4 + y) * WIDTH * 4
            fin[at:at + 4 * PAIRS] = w[y]
            fin[at + 4 * PAIRS:at + 8 * PAIRS] = turned

    def do_spread(j):
        contract(j)

        @pl.loop(0, planes - 1)
        def _(i):
            k = i // 4
            z = lax.rem(zn // 2 + (k + 1) // 2 * (1 - 2 * lax.rem(k, 2)) + zn, zn)
            spread(j, 4 * z + 3 - lax.rem(i, 4)).start()

        zr[j, gx] = p[j, gx]

    def await_part(n):
        size = slice(0, 11 * WIDTH * 16 // (2 if n < 2 else 1))
        wait(dummy.at[size], x_r.at[n])

    def first(part):
        @pl.loop(4 * part, 4 * part + 4)
        def _(i):
            first_of(i)

    entered = lambda: pl.semaphore_wait(barrier, 1 + 15 + (zn - 1))
    for part in range(4):
        first(part)
        if part == 1:
            load_x.wait()
            entered()
            for n in range(part):
                swap(n).start()
        if part >= 1:
            swap(part).start()
        if part == 1:
            @pl.loop(1, 4)
            def _(d):
                gather_fx(d).start()
        if part == 2:
            second_of(0)
            second_of(1)
            send_relay(parts[0])
            send_plain(parts[0])
    second_of(2)
    second_of(3)
    send_relay(parts[1])
    send_plain(parts[1])
    rx[0, 4 + yi] = t3[rows(plane * WIDTH * 16, WIDTH * 16)]
    for j in range(1, CHUNKS):
        rx[j, 4 + yi] = t3[rows((j * 16 + plane) * WIDTH * 16, WIDTH * 16)]
    send_merged(parts[0])
    send_relay(parts[2])
    send_merged(parts[1])
    for j in range(1, CHUNKS):
        send_plain(parts[1 + j])
        if j == 1:
            wait(fxg.at[0:96], g_r)
            fxl[...] = stacked(fxg[...].T)
        if j + 1 < CHUNKS:
            send_relay(parts[2 + j])
        send_merged(parts[1 + j])
    for j in range(CHUNKS):
        if j == 0:
            await_part(0)
            await_part(1)
        else:
            await_part(j + 1)
        do_spread(j)
    for j in range(CHUNKS):
        wait(zr.at[j, 0:planes - 1], z_r.at[j])
        total(j)
    for a in range(4):
        out[a] = fin[pl.ds(a, 32, stride=4), :][:, :64]

    for n in range(4):
        swap(n).wait_send()
    wait(fxg.at[0:96], g_s)
    for n, part in enumerate(parts):
        for way in range(2):
            relay(part, way).wait_send()
        wait(dummy.at[0:11 * WIDTH * 16 // (2 if n < 2 else 1)], x_s.at[n])
    for j in range(CHUNKS):
        wait(zr.at[j, 0:planes - 1], z_s.at[j])


def body(zn, snapshot, factor_x, factor_y, factor_z):
    anywhere = pl.BlockSpec(memory_space=pl.ANY)
    dma = pltpu.SemaphoreType.DMA
    core = pl.pallas_call(
        functools.partial(kernel, zn),
        out_shape=pltpu.VMEM((4, 32, 64), F32),
        in_specs=[anywhere] * 4,
        out_specs=pl.BlockSpec(memory_space=pltpu.VMEM),
        scratch_shapes=[
            pltpu.VMEM((16, 2, 256, 128), F32),
            pltpu.VMEM((256, 128), F32),
            pltpu.VMEM((128, 128), F32),
            pltpu.VMEM((128, 128), F32),
            pltpu.VMEM((128, 256), F32),
            pltpu.VMEM((256, 256), BF16),
            pltpu.VMEM((256, 256), BF16),
            pltpu.VMEM((256, 256), BF16),
            pltpu.VMEM((16, 128, 128), F32),
            pltpu.VMEM((16, 128, 128), F32),
            pltpu.VMEM((16, 128, 128), F32),
            pltpu.VMEM((2048, 128), F32),
            pltpu.VMEM((CHUNKS, 12, WIDTH * 16, 128), F32),
            pltpu.VMEM((CHUNKS, 2, WIDTH * 32, 128), F32),
            pltpu.VMEM((CHUNKS, 4 * zn, 4 * PAIRS, 128), F32),
            pltpu.VMEM((CHUNKS, 4 * zn, 4 * PAIRS, 128), F32),
            pltpu.VMEM((128, 128), F32),
            dma((16,)), dma((3,)), dma((4,)), dma((4,)),
            dma((1 + CHUNKS, 2)), dma((1 + CHUNKS, 2)), dma((1 + CHUNKS,)), dma((1 + CHUNKS,)), dma((CHUNKS,)), dma((CHUNKS,)), dma, dma,
        ],
        compiler_params=pltpu.CompilerParams(
            collective_id=0, has_side_effects=True, vmem_limit_bytes=40 * 1024 * 1024
        ),
    )(*(pltpu.with_memory_space_constraint(a, pltpu.HBM) for a in (snapshot.reshape(2, 16, 256, 128), factor_x, factor_y, factor_z)))
    return core.transpose(0, 2, 1)


def solution(mesh):
    return jax.shard_map(
        functools.partial(body, mesh.shape["gx"] // 4),
        mesh=mesh,
        in_specs=(P("gx", "gy", "gz"), P("gx", None), P("gy", None), P("gz", None)),
        out_specs=P("gx", "gy", "gz"),
        check_vma=False,
    )
```

```python
import functools

import jax
import jax.numpy as jnp
from jax import lax
from jax.experimental import pallas as pl
from jax.experimental.pallas import tpu as pltpu
from jax.sharding import PartitionSpec as P

MESH = pl.DeviceIdType.MESH
F32, BF16 = jnp.float32, jnp.bfloat16
NT = (((1,), (1,)), ((), ()))
CHUNKS = 2
WIDTH = 8 // CHUNKS
PAIRS = WIDTH // 2


def split(value):
    high = value.astype(BF16)
    return high, (value - high.astype(F32)).astype(BF16)


def rows(start, size):
    return pl.ds(pl.multiple_of(start, 8), size)


def stacked(factor_t):
    high, low = split(factor_t)
    top = jnp.concatenate([high, high], axis=1)
    return jnp.concatenate([top, jnp.concatenate([low, jnp.zeros_like(low)], axis=1)], axis=0)


def kernel(
    zn, snap, fx, fy, fz, out,
    s_buf, fy_v, fz_v, fxg, ft, fyl, fzl, fxl, t1s, t1o, t1r, t3, rx, rx1, p, zr, fin,
    s_sem, f_sem, ys, yr, r_s, r_r, x_s, x_r, z_s, z_r, g_s, g_r, known,
):
    gx, core, xi = lax.axis_index("gx"), lax.axis_index("gy"), lax.axis_index("gz")
    zi, yi = gx // 4, lax.rem(gx, 4)
    other = 1 - core
    plane = xi * 4 + yi
    planes = 4 * zn

    right, opposite, left = lax.rem(xi + 1, 4), lax.rem(xi + 2, 4), lax.rem(xi + 3, 4)

    def in_column(d):
        z, y = lax.rem(zi + d // 4, zn), lax.rem(yi + lax.rem(d, 4), 4)
        return z * 4 + y, (z * 4 + y, core, xi)

    def load(i):
        return pltpu.make_async_copy(snap.at[:, i], s_buf.at[i], s_sem.at[i])

    load_y = pltpu.make_async_copy(fy, fy_v, f_sem.at[0])
    load_z = pltpu.make_async_copy(fz, fz_v, f_sem.at[1])
    my_fx = fxg.at[rows(yi * 32, 32)]
    load_x = pltpu.make_async_copy(fx, my_fx, f_sem.at[2])
    load_y.start()
    load_z.start()
    load_x.start()

    @pl.loop(0, 16)
    def _(i):
        load(i).start()


    barrier = pltpu.get_barrier_semaphore()
    pl.semaphore_signal(barrier, inc=1, device_id=(gx, other, xi), device_id_type=MESH)

    for x in (left, right):
        pl.semaphore_signal(barrier, inc=1, device_id=(gx, core, x), device_id_type=MESH)

    @pl.loop(1, 4)
    def _(d):
        pl.semaphore_signal(barrier, inc=1, device_id=in_column(d)[1], device_id_type=MESH)

    for d in (1, zn - 1):
        pl.semaphore_signal(barrier, inc=1, device_id=in_column(4 * d)[1], device_id_type=MESH)

    def tell_x(stage):
        for x in (left, right):
            pl.semaphore_signal(known.at[stage], inc=1, device_id=(gx, core, x), device_id_type=MESH)

    def tell_y(stage):
        @pl.loop(1, 4)
        def _(d):
            pl.semaphore_signal(known.at[stage], inc=1, device_id=in_column(d)[1], device_id_type=MESH)

    def tell_z(stage, distance):
        for d in (distance, zn - distance):
            pl.semaphore_signal(known.at[stage], inc=1, device_id=in_column(4 * d)[1], device_id_type=MESH)

    load_y.wait()
    ft[...] = fy_v[...].T
    high, low = split(jnp.concatenate([ft[rows(other * 64, 64)], ft[rows(core * 64, 64)]], axis=0))
    fyl[...] = jnp.concatenate([high, low], axis=0)
    def first(part):
        for i in range(4 * part, 4 * part + 4):
            load(i).wait()
        for i in range(4 * part, 4 * part + 4):
            high, low = split(jnp.concatenate([s_buf[i, 0], s_buf[i, 1]], axis=1))
            both = jnp.dot(fyl[...], high, preferred_element_type=F32)
            t = both[:128] + both[128:] + jnp.dot(fyl[0:128], low, preferred_element_type=F32)
            for h in range(2):
                piece = t[:, 128 * h:128 * h + 128]
                t1s[i, 64 * h:64 * h + 64] = piece[:64]
                t1o[i, 64 * h:64 * h + 64] = piece[64:]

    def swap(part):
        at = pl.ds(4 * part, 4)
        return pltpu.make_async_remote_copy(
            src_ref=t1s.at[at], dst_ref=t1r.at[at], send_sem=ys.at[part], recv_sem=yr.at[part],
            device_id=(gx, other, xi), device_id_type=MESH)

    def second_of(part):
        swap(part).wait_recv()
        for i in range(2):
            n = 4 * part + 2 * i
            t2 = (t1o[n:n + 2] + t1r[n:n + 2]).reshape(256, 128)
            w = jnp.concatenate(split(t2), axis=1)
            q = lax.dot_general(fzl[...], w, NT, preferred_element_type=F32)
            q = q[:128] + q[128:]
            t3[pl.ds(n, 128, stride=16), :] = q[:, :128]
            t3[pl.ds(n + 1, 128, stride=16), :] = q[:, 128:]

    def block_of(part, x, y, number):
        j, h = part[:2]
        at = ((j * 4 + x) * 4 + y) * WIDTH
        if h is None:
            return t3.at[pl.ds(pl.multiple_of(at * 16, 32), number * 16)]
        return t3.reshape(128, 2, 8, 128).at[pl.ds(at, number), h]

    def slot_of(ref, part, at):
        j, h = part[:2]
        if h is None:
            return ref.at[j, at]
        return ref.reshape(*ref.shape[:-2], ref.shape[-2] // 16, 2, 8, 128).at[j, at, :, h]

    def relay(part, way):
        return pltpu.make_async_remote_copy(
            src_ref=block_of(part, opposite, 2 * way, 2 * WIDTH), dst_ref=slot_of(rx1, part, way),
            send_sem=r_s.at[part[2], way], recv_sem=r_r.at[part[2], way],
            device_id=(gx, core, (right, left)[way]), device_id_type=MESH)

    def send_relay(part):
        for way in range(2):
            relay(part, way).start()

    def exchange(part, x, y, slot):
        pltpu.make_async_remote_copy(
            src_ref=block_of(part, x, y, WIDTH), dst_ref=slot_of(rx, part, slot * 4 + yi),
            send_sem=x_s.at[part[2]], recv_sem=x_r.at[part[2]],
            device_id=(zi * 4 + y, core, x), device_id_type=MESH).start()

    def send_plain(part):
        @pl.loop(1, 4)
        def _(d):
            exchange(part, xi, lax.rem(yi + d, 4), 1)

        @pl.loop(0, 2)
        def _(y):
            exchange(part, right, y + 2, 0)
            exchange(part, left, y, 2)

    def send_merged(part):
        for way in range(2):
            relay(part, way).wait_recv()
            to = block_of(part, (right, left)[way], 2 * way, 2 * WIDTH)
            to[...] = to[...] + slot_of(rx1, part, way)[...]

        @pl.loop(0, 2)
        def _(y):
            exchange(part, right, y, 0)
            exchange(part, left, y + 2, 2)

    def spread(j, d):
        block, to = in_column(d)
        return pltpu.make_async_remote_copy(
            src_ref=p.at[j, block], dst_ref=zr.at[j, gx],
            send_sem=z_s.at[j], recv_sem=z_r.at[j], device_id=to, device_id_type=MESH)

    def gather_fx(d):
        y = lax.rem(yi + d, 4)
        return pltpu.make_async_remote_copy(
            src_ref=my_fx, dst_ref=my_fx, send_sem=g_s, recv_sem=g_r,
            device_id=(zi * 4 + y, core, xi), device_id_type=MESH)

    dummy = t3

    def wait(ref, sem):
        pltpu.make_async_copy(ref, ref, sem).wait()

    parts = [(0, 0, 0), (0, 1, 1)] + [(j, None, 1 + j) for j in range(1, CHUNKS)]

    def contract(j):
        add = rx[j, 0:4] + rx[j, 4:8] + rx[j, 8:12]
        turned = pltpu.roll(add.reshape(-1, 128), 64, 1).reshape(add.shape)
        low_half = lax.broadcasted_iota(jnp.int32, (16, 128), 1) < 64
        columns = []
        for q in range(PAIRS):
            c0, c1 = slice(16 * q, 16 * q + 16), slice(16 * (PAIRS + q), 16 * (PAIRS + q) + 16)
            pieces = []
            for y in range(4):
                pieces.append(jnp.where(low_half, add[y, c0], turned[y, c1]))
                pieces.append(jnp.where(low_half, turned[y, c0], add[y, c1]))
            columns.append(jnp.concatenate(pieces, axis=0))
        w = jnp.concatenate(split(jnp.concatenate(columns, axis=1)), axis=0)
        r = jnp.dot(fxl[...], w, preferred_element_type=F32)
        r = r[:128] + r[128:]
        for q in range(PAIRS):
            p[j, :, 4 * q:4 * q + 4] = r[:, 128 * q:128 * q + 128].reshape(planes, 4, 128)

    def total(j):
        w = zr[j, 0:4]
        for z in range(1, zn):
            w = w + zr[j, 4 * z:4 * z + 4]
        for y in range(4):
            turned = pltpu.roll(w[y], 64, 1)
            at = (j * 4 + y) * WIDTH * 4
            fin[at:at + 4 * PAIRS] = w[y]
            fin[at + 4 * PAIRS:at + 8 * PAIRS] = turned

    def do_spread(j):
        contract(j)

        @pl.loop(0, planes - 1)
        def _(i):
            k = i // 4
            z = lax.rem(zn // 2 + (k + 1) // 2 * (1 - 2 * lax.rem(k, 2)) + zn, zn)
            spread(j, 4 * z + 3 - lax.rem(i, 4)).start()

        zr[j, gx] = p[j, gx]

    def await_part(n):
        size = slice(0, 11 * WIDTH * 16 // (2 if n < 2 else 1))
        wait(dummy.at[size], x_r.at[n])

    entered = lambda: pl.semaphore_wait(barrier, 8)
    for part in range(4):
        first(part)
        if part == 1:
            load_z.wait()
            group = 4 * WIDTH
            fz_t = fz_v[...].T
            fzl[...] = stacked(jnp.concatenate(
                [fz_t[32 * x + group * j:32 * x + group * (j + 1)] for j in range(CHUNKS) for x in range(4)], axis=0))
            load_x.wait()
            entered()
            for n in range(part):
                swap(n).start()
            tell_x(0)
            tell_z(1, 1)
        if part >= 1:
            swap(part).start()
        if part == 1:
            @pl.loop(1, 4)
            def _(d):
                gather_fx(d).start()
        if part == 2:
            second_of(0)
            second_of(1)
            send_relay(parts[0])
            pl.semaphore_wait(known.at[0], 2)
            send_plain(parts[0])
    second_of(2)
    second_of(3)
    send_relay(parts[1])
    send_plain(parts[1])
    pl.semaphore_wait(known.at[1], 2)
    tell_z(2, 2)
    rx[0, 4 + yi] = t3[rows(plane * WIDTH * 16, WIDTH * 16)]
    for j in range(1, CHUNKS):
        rx[j, 4 + yi] = t3[rows((j * 16 + plane) * WIDTH * 16, WIDTH * 16)]
    send_merged(parts[0])
    send_relay(parts[2])
    send_merged(parts[1])
    pl.semaphore_wait(known.at[2], 2)
    tell_y(3)
    for j in range(1, CHUNKS):
        send_plain(parts[1 + j])
        if j == 1:
            wait(fxg.at[0:96], g_r)
            fxl[...] = stacked(fxg[...].T)
        if j + 1 < CHUNKS:
            send_relay(parts[2 + j])
        send_merged(parts[1 + j])
    pl.semaphore_wait(known.at[3], 3)
    for j in range(CHUNKS):
        if j == 0:
            await_part(0)
            await_part(1)
        else:
            await_part(j + 1)
        do_spread(j)
    for n in range(4):
        swap(n).wait_send()
    wait(fxg.at[0:96], g_s)
    for n, part in enumerate(parts):
        for way in range(2):
            relay(part, way).wait_send()
        wait(dummy.at[0:11 * WIDTH * 16 // (2 if n < 2 else 1)], x_s.at[n])
    for j in range(CHUNKS):
        wait(zr.at[j, 0:planes - 1], z_r.at[j])
        total(j)
    for a in range(4):
        out[a] = fin[pl.ds(a, 32, stride=4), :][:, :64]

    for j in range(CHUNKS):
        wait(zr.at[j, 0:planes - 1], z_s.at[j])


def body(zn, snapshot, factor_x, factor_y, factor_z):
    anywhere = pl.BlockSpec(memory_space=pl.ANY)
    dma = pltpu.SemaphoreType.DMA
    core = pl.pallas_call(
        functools.partial(kernel, zn),
        out_shape=pltpu.VMEM((4, 32, 64), F32),
        in_specs=[anywhere] * 4,
        out_specs=pl.BlockSpec(memory_space=pltpu.VMEM),
        scratch_shapes=[
            pltpu.VMEM((16, 2, 256, 128), F32),
            pltpu.VMEM((256, 128), F32),
            pltpu.VMEM((128, 128), F32),
            pltpu.VMEM((128, 128), F32),
            pltpu.VMEM((128, 256), F32),
            pltpu.VMEM((256, 256), BF16),
            pltpu.VMEM((256, 256), BF16),
            pltpu.VMEM((256, 256), BF16),
            pltpu.VMEM((16, 128, 128), F32),
            pltpu.VMEM((16, 128, 128), F32),
            pltpu.VMEM((16, 128, 128), F32),
            pltpu.VMEM((2048, 128), F32),
            pltpu.VMEM((CHUNKS, 12, WIDTH * 16, 128), F32),
            pltpu.VMEM((CHUNKS, 2, WIDTH * 32, 128), F32),
            pltpu.VMEM((CHUNKS, 4 * zn, 4 * PAIRS, 128), F32),
            pltpu.VMEM((CHUNKS, 4 * zn, 4 * PAIRS, 128), F32),
            pltpu.VMEM((128, 128), F32),
            dma((16,)), dma((3,)), dma((4,)), dma((4,)),
            dma((1 + CHUNKS, 2)), dma((1 + CHUNKS, 2)), dma((1 + CHUNKS,)), dma((1 + CHUNKS,)), dma((CHUNKS,)), dma((CHUNKS,)), dma, dma,
            pltpu.SemaphoreType.REGULAR((4,)),
        ],
        compiler_params=pltpu.CompilerParams(
            collective_id=0, has_side_effects=True, vmem_limit_bytes=40 * 1024 * 1024
        ),
    )(*(pltpu.with_memory_space_constraint(a, pltpu.HBM) for a in (snapshot.reshape(2, 16, 256, 128), factor_x, factor_y, factor_z)))
    return core.transpose(0, 2, 1)


def solution(mesh):
    return jax.shard_map(
        functools.partial(body, mesh.shape["gx"] // 4),
        mesh=mesh,
        in_specs=(P("gx", "gy", "gz"), P("gx", None), P("gy", None), P("gz", None)),
        out_specs=P("gx", "gy", "gz"),
        check_vma=False,
    )
```

```python
import functools

import jax
import jax.numpy as jnp
from jax import lax
from jax.experimental import pallas as pl
from jax.experimental.pallas import tpu as pltpu
from jax.sharding import PartitionSpec as P

MESH = pl.DeviceIdType.MESH
F32, BF16 = jnp.float32, jnp.bfloat16
NT = (((1,), (1,)), ((), ()))
CHUNKS = 2
WIDTH = 8 // CHUNKS
PAIRS = WIDTH // 2


def split(value):
    high = value.astype(BF16)
    return high, (value - high.astype(F32)).astype(BF16)


def rows(start, size):
    return pl.ds(pl.multiple_of(start, 8), size)


def stacked(factor_t):
    high, low = split(factor_t)
    top = jnp.concatenate([high, high], axis=1)
    return jnp.concatenate([top, jnp.concatenate([low, jnp.zeros_like(low)], axis=1)], axis=0)


def kernel(
    zn, snap, fx, fy, fz, out,
    s_buf, fy_v, fz_v, fxg, ft, fyl, fzl, fxl, t1s, t1o, t1r, t3, rx, rx1, p, zr, fin,
    s_sem, f_sem, ys, yr, r_s, r_r, x_s, x_r, z_s, z_r, g_s, g_r, known,
):
    gx, core, xi = lax.axis_index("gx"), lax.axis_index("gy"), lax.axis_index("gz")
    zi, yi = gx // 4, lax.rem(gx, 4)
    other = 1 - core
    plane = xi * 4 + yi
    planes = 4 * zn

    right, opposite, left = lax.rem(xi + 1, 4), lax.rem(xi + 2, 4), lax.rem(xi + 3, 4)

    def in_column(d):
        z, y = lax.rem(zi + d // 4, zn), lax.rem(yi + lax.rem(d, 4), 4)
        return z * 4 + y, (z * 4 + y, core, xi)

    def load(i):
        return pltpu.make_async_copy(snap.at[:, i], s_buf.at[i], s_sem.at[i])

    load_y = pltpu.make_async_copy(fy, fy_v, f_sem.at[0])
    load_z = pltpu.make_async_copy(fz, fz_v, f_sem.at[1])
    my_fx = fxg.at[rows(yi * 32, 32)]
    load_x = pltpu.make_async_copy(fx, my_fx, f_sem.at[2])
    load_y.start()
    load_z.start()
    load_x.start()

    @pl.loop(0, 16)
    def _(i):
        load(i).start()

    barrier = pltpu.get_barrier_semaphore()
    pl.semaphore_signal(barrier, inc=1, device_id=(gx, other, xi), device_id_type=MESH)

    for x in (left, right):
        pl.semaphore_signal(barrier, inc=1, device_id=(gx, core, x), device_id_type=MESH)

    @pl.loop(1, 4)
    def _(d):
        pl.semaphore_signal(barrier, inc=1, device_id=in_column(d)[1], device_id_type=MESH)

    for d in (1, zn - 1):
        pl.semaphore_signal(barrier, inc=1, device_id=in_column(4 * d)[1], device_id_type=MESH)

    def tell_x(stage):
        for x in (left, right):
            pl.semaphore_signal(known.at[stage], inc=1, device_id=(gx, core, x), device_id_type=MESH)

    def tell_y(stage):
        @pl.loop(1, 4)
        def _(d):
            pl.semaphore_signal(known.at[stage], inc=1, device_id=in_column(d)[1], device_id_type=MESH)

    def tell_z(stage, distance):
        for d in (distance, zn - distance):
            pl.semaphore_signal(known.at[stage], inc=1, device_id=in_column(4 * d)[1], device_id_type=MESH)

    load_y.wait()
    ft[...] = fy_v[...].T
    high, low = split(jnp.concatenate([ft[rows(other * 64, 64)], ft[rows(core * 64, 64)]], axis=0))
    fyl[...] = jnp.concatenate([high, low], axis=0)
    def first(part):
        for i in range(4 * part, 4 * part + 4):
            load(i).wait()
        for i in range(4 * part, 4 * part + 4):
            high, low = split(jnp.concatenate([s_buf[i, 0], s_buf[i, 1]], axis=1))
            both = jnp.dot(fyl[...], high, preferred_element_type=F32)
            t = both[:128] + both[128:] + jnp.dot(fyl[0:128], low, preferred_element_type=F32)
            for h in range(2):
                piece = t[:, 128 * h:128 * h + 128]
                t1s[i, 64 * h:64 * h + 64] = piece[:64]
                t1o[i, 64 * h:64 * h + 64] = piece[64:]

    def swap(part):
        at = pl.ds(4 * part, 4)
        return pltpu.make_async_remote_copy(
            src_ref=t1s.at[at], dst_ref=t1r.at[at], send_sem=ys.at[part], recv_sem=yr.at[part],
            device_id=(gx, other, xi), device_id_type=MESH)

    def second_of(part):
        swap(part).wait_recv()
        for i in range(2):
            n = 4 * part + 2 * i
            t2 = (t1o[n:n + 2] + t1r[n:n + 2]).reshape(256, 128)
            w = jnp.concatenate(split(t2), axis=1)
            q = lax.dot_general(fzl[...], w, NT, preferred_element_type=F32)
            q = q[:128] + q[128:]
            t3[pl.ds(n, 128, stride=16), :] = q[:, :128]
            t3[pl.ds(n + 1, 128, stride=16), :] = q[:, 128:]

    def block_of(part, x, y, number):
        j, h = part[:2]
        at = ((j * 4 + x) * 4 + y) * WIDTH
        if h is None:
            return t3.at[pl.ds(pl.multiple_of(at * 16, 32), number * 16)]
        return t3.reshape(129, 2, 8, 128).at[pl.ds(at, number), h]

    def slot_of(ref, part, at):
        j, h = part[:2]
        if h is None:
            return ref.at[j, at]
        return ref.reshape(*ref.shape[:-2], ref.shape[-2] // 16, 2, 8, 128).at[j, at, :, h]

    def relay(part, way):
        return pltpu.make_async_remote_copy(
            src_ref=block_of(part, opposite, 2 * way, 2 * WIDTH), dst_ref=slot_of(rx1, part, way),
            send_sem=r_s.at[part[2], way], recv_sem=r_r.at[part[2], way],
            device_id=(gx, core, (right, left)[way]), device_id_type=MESH)

    def send_relay(part):
        for way in range(2):
            relay(part, way).start()

    def exchange(part, x, y, slot):
        pltpu.make_async_remote_copy(
            src_ref=block_of(part, x, y, WIDTH), dst_ref=slot_of(rx, part, slot * 4 + yi),
            send_sem=x_s.at[part[2]], recv_sem=x_r.at[part[2]],
            device_id=(zi * 4 + y, core, x), device_id_type=MESH).start()

    def send_plain(part):
        @pl.loop(1, 4)
        def _(d):
            exchange(part, xi, lax.rem(yi + d, 4), 1)

        @pl.loop(0, 2)
        def _(y):
            exchange(part, right, y + 2, 0)
            exchange(part, left, y, 2)

    def send_merged(part):
        for way in range(2):
            relay(part, way).wait_recv()
            to = block_of(part, (right, left)[way], 2 * way, 2 * WIDTH)
            to[...] = to[...] + slot_of(rx1, part, way)[...]

        @pl.loop(0, 2)
        def _(y):
            exchange(part, right, y, 0)
            exchange(part, left, y + 2, 2)

    def spread(j, d):
        block, to = in_column(d)
        return pltpu.make_async_remote_copy(
            src_ref=p.at[j, block], dst_ref=zr.at[j, gx],
            send_sem=z_s.at[j], recv_sem=z_r.at[j], device_id=to, device_id_type=MESH)

    def gather_fx(d):
        y = lax.rem(yi + d, 4)
        return pltpu.make_async_remote_copy(
            src_ref=my_fx, dst_ref=my_fx, send_sem=g_s, recv_sem=g_r,
            device_id=(zi * 4 + y, core, xi), device_id_type=MESH)

    dummy = t3

    def wait(ref, sem):
        pltpu.make_async_copy(ref, ref, sem).wait()

    parts = [(0, 0, 0), (0, 1, 1)] + [(j, None, 1 + j) for j in range(1, CHUNKS)]

    def contract(j):
        add = rx[j, 0:4] + rx[j, 4:8] + rx[j, 8:12]
        turned = pltpu.roll(add.reshape(-1, 128), 64, 1).reshape(add.shape)
        low_half = lax.broadcasted_iota(jnp.int32, (16, 128), 1) < 64
        columns = []
        for q in range(PAIRS):
            c0, c1 = slice(16 * q, 16 * q + 16), slice(16 * (PAIRS + q), 16 * (PAIRS + q) + 16)
            pieces = []
            for y in range(4):
                pieces.append(jnp.where(low_half, add[y, c0], turned[y, c1]))
                pieces.append(jnp.where(low_half, turned[y, c0], add[y, c1]))
            columns.append(jnp.concatenate(pieces, axis=0))
        w = jnp.concatenate(split(jnp.concatenate(columns, axis=1)), axis=0)
        r = jnp.dot(fxl[...], w, preferred_element_type=F32)
        r = r[:128] + r[128:]
        for q in range(PAIRS):
            p[j, :, 4 * q:4 * q + 4] = r[:, 128 * q:128 * q + 128].reshape(planes, 4, 128)

    def total(j):
        w = zr[j, 0:4]
        for z in range(1, zn):
            w = w + zr[j, 4 * z:4 * z + 4]
        for y in range(4):
            turned = pltpu.roll(w[y], 64, 1)
            at = (j * 4 + y) * WIDTH * 4
            fin[at:at + 4 * PAIRS] = w[y]
            fin[at + 4 * PAIRS:at + 8 * PAIRS] = turned

    def do_spread(j):
        contract(j)

        @pl.loop(0, planes - 1)
        def _(i):
            k = i // 4
            z = lax.rem(zn // 2 + (k + 1) // 2 * (1 - 2 * lax.rem(k, 2)) + zn, zn)
            spread(j, 4 * z + 3 - lax.rem(i, 4)).start()

        zr[j, gx] = p[j, gx]

    def await_part(n):
        size = slice(0, 11 * WIDTH * 16 // (2 if n < 2 else 1))
        wait(dummy.at[size], x_r.at[n])

    entered = lambda: pl.semaphore_wait(barrier, 8)
    for part in range(4):
        first(part)
        if part == 0:
            load_z.wait()
            group = 4 * WIDTH
            fz_t = fz_v[...].T
            fzl[...] = stacked(jnp.concatenate(
                [fz_t[32 * x + group * j:32 * x + group * (j + 1)] for j in range(CHUNKS) for x in range(4)], axis=0))
            load_x.wait()
            entered()
            for n in range(part):
                swap(n).start()
            tell_x(0)
            tell_z(1, 1)
        swap(part).start()
        if part == 1:
            @pl.loop(1, 4)
            def _(d):
                gather_fx(d).start()
        if part == 2:
            second_of(0)
            second_of(1)
            send_relay(parts[0])
            pl.semaphore_wait(known.at[0], 2)
            send_plain(parts[0])
    second_of(2)
    second_of(3)
    send_relay(parts[1])
    send_plain(parts[1])
    pl.semaphore_wait(known.at[1], 2)
    tell_z(2, 2)
    rx[0, 4 + yi] = t3[rows(plane * WIDTH * 16, WIDTH * 16)]
    for j in range(1, CHUNKS):
        rx[j, 4 + yi] = t3[rows((j * 16 + plane) * WIDTH * 16, WIDTH * 16)]
    send_merged(parts[0])
    send_relay(parts[2])
    send_merged(parts[1])
    pl.semaphore_wait(known.at[2], 2)
    tell_y(3)
    for j in range(1, CHUNKS):
        send_plain(parts[1 + j])
        if j == 1:
            wait(fxg.at[0:96], g_r)
            fxl[...] = stacked(fxg[...].T)
        if j + 1 < CHUNKS:
            send_relay(parts[2 + j])
        send_merged(parts[1 + j])
    pl.semaphore_wait(known.at[3], 3)
    for j in range(CHUNKS):
        if j == 0:
            await_part(0)
            await_part(1)
        else:
            await_part(j + 1)
        do_spread(j)
    for n in range(4):
        swap(n).wait_send()
    wait(fxg.at[0:96], g_s)
    for n, part in enumerate(parts):
        for way in range(2):
            relay(part, way).wait_send()
        wait(dummy.at[0:11 * WIDTH * 16 // (2 if n < 2 else 1)], x_s.at[n])
    for j in range(CHUNKS):
        wait(zr.at[j, 0:planes - 1], z_r.at[j])
        total(j)
    for a in range(4):
        out[a] = fin[pl.ds(a, 32, stride=4), :][:, :64]

    for j in range(CHUNKS):
        wait(zr.at[j, 0:planes - 1], z_s.at[j])


def body(zn, snapshot, factor_x, factor_y, factor_z):
    anywhere = pl.BlockSpec(memory_space=pl.ANY)
    dma = pltpu.SemaphoreType.DMA
    core = pl.pallas_call(
        functools.partial(kernel, zn),
        out_shape=pltpu.VMEM((4, 32, 64), F32),
        in_specs=[anywhere] * 4,
        out_specs=pl.BlockSpec(memory_space=pltpu.VMEM),
        scratch_shapes=[
            pltpu.VMEM((16, 2, 256, 128), F32),
            pltpu.VMEM((256, 128), F32),
            pltpu.VMEM((128, 128), F32),
            pltpu.VMEM((128, 128), F32),
            pltpu.VMEM((128, 256), F32),
            pltpu.VMEM((256, 256), BF16),
            pltpu.VMEM((256, 256), BF16),
            pltpu.VMEM((256, 256), BF16),
            pltpu.VMEM((16, 128, 128), F32),
            pltpu.VMEM((16, 128, 128), F32),
            pltpu.VMEM((16, 128, 128), F32),
            pltpu.VMEM((2064, 128), F32),
            pltpu.VMEM((CHUNKS, 12, WIDTH * 16, 128), F32),
            pltpu.VMEM((CHUNKS, 2, WIDTH * 32, 128), F32),
            pltpu.VMEM((CHUNKS, 4 * zn, 4 * PAIRS, 128), F32),
            pltpu.VMEM((CHUNKS, 4 * zn, 4 * PAIRS, 128), F32),
            pltpu.VMEM((136, 128), F32),
            dma((16,)), dma((3,)), dma((4,)), dma((4,)),
            dma((1 + CHUNKS, 2)), dma((1 + CHUNKS, 2)), dma((1 + CHUNKS,)), dma((1 + CHUNKS,)), dma((CHUNKS,)), dma((CHUNKS,)), dma, dma,
            pltpu.SemaphoreType.REGULAR((4,)),
        ],
        compiler_params=pltpu.CompilerParams(
            collective_id=0, has_side_effects=True, vmem_limit_bytes=40 * 1024 * 1024
        ),
    )(*(pltpu.with_memory_space_constraint(a, pltpu.HBM) for a in (snapshot.reshape(2, 16, 256, 128), factor_x, factor_y, factor_z)))
    return core.transpose(0, 2, 1)


def solution(mesh):
    return jax.shard_map(
        functools.partial(body, mesh.shape["gx"] // 4),
        mesh=mesh,
        in_specs=(P("gx", "gy", "gz"), P("gx", None), P("gy", None), P("gz", None)),
        out_specs=P("gx", "gy", "gz"),
        check_vma=False,
    )
```

```python
import functools

import jax
import jax.numpy as jnp
from jax import lax
from jax.experimental import pallas as pl
from jax.experimental.pallas import tpu as pltpu
from jax.sharding import PartitionSpec as P

MESH = pl.DeviceIdType.MESH
F32, BF16 = jnp.float32, jnp.bfloat16
NT = (((1,), (1,)), ((), ()))
CHUNKS = 2
WIDTH = 8 // CHUNKS
PAIRS = WIDTH // 2


def split(value):
    high = value.astype(BF16)
    return high, (value - high.astype(F32)).astype(BF16)


def rows(start, size):
    return pl.ds(pl.multiple_of(start, 8), size)


def stacked(factor_t):
    high, low = split(factor_t)
    top = jnp.concatenate([high, high], axis=1)
    return jnp.concatenate([top, jnp.concatenate([low, jnp.zeros_like(low)], axis=1)], axis=0)


def kernel(
    zn, snap, fx, fy, fz, out,
    s_buf, fy_v, fz_v, fxg, ft, fyl, fzl, fxl, t1s, t1o, t1r, t3, rx, rx1, p, zr, fin,
    s_sem, f_sem, ys, yr, r_s, r_r, x_s, x_r, z_s, z_r, g_s, g_r, known,
):
    gx, core, xi = lax.axis_index("gx"), lax.axis_index("gy"), lax.axis_index("gz")
    zi, yi = gx // 4, lax.rem(gx, 4)
    other = 1 - core
    plane = xi * 4 + yi
    planes = 4 * zn

    right, opposite, left = lax.rem(xi + 1, 4), lax.rem(xi + 2, 4), lax.rem(xi + 3, 4)

    def in_column(d):
        z, y = lax.rem(zi + d // 4, zn), lax.rem(yi + lax.rem(d, 4), 4)
        return z * 4 + y, (z * 4 + y, core, xi)

    def load(i):
        return pltpu.make_async_copy(snap.at[:, i], s_buf.at[i], s_sem.at[i])

    load_y = pltpu.make_async_copy(fy, fy_v, f_sem.at[0])
    load_z = pltpu.make_async_copy(fz, fz_v, f_sem.at[1])
    my_fx = fxg.at[rows(yi * 32, 32)]
    load_x = pltpu.make_async_copy(fx, my_fx, f_sem.at[2])
    load_y.start()
    load_z.start()
    load_x.start()

    @pl.loop(0, 16)
    def _(i):
        load(i).start()

    barrier = pltpu.get_barrier_semaphore()
    pl.semaphore_signal(barrier, inc=1, device_id=(gx, other, xi), device_id_type=MESH)

    for x in (left, right):
        pl.semaphore_signal(barrier, inc=1, device_id=(gx, core, x), device_id_type=MESH)

    @pl.loop(1, 4)
    def _(d):
        pl.semaphore_signal(barrier, inc=1, device_id=in_column(d)[1], device_id_type=MESH)

    for d in (1, zn - 1):
        pl.semaphore_signal(barrier, inc=1, device_id=in_column(4 * d)[1], device_id_type=MESH)

    def tell_x(stage):
        for x in (left, right):
            pl.semaphore_signal(known.at[stage], inc=1, device_id=(gx, core, x), device_id_type=MESH)

    def tell_y(stage):
        @pl.loop(1, 4)
        def _(d):
            pl.semaphore_signal(known.at[stage], inc=1, device_id=in_column(d)[1], device_id_type=MESH)

    def tell_z(stage, distance):
        for d in (distance, zn - distance):
            pl.semaphore_signal(known.at[stage], inc=1, device_id=in_column(4 * d)[1], device_id_type=MESH)

    load_y.wait()
    ft[...] = fy_v[...].T
    high, low = split(jnp.concatenate([ft[rows(other * 64, 64)], ft[rows(core * 64, 64)]], axis=0))
    fyl[...] = jnp.concatenate([high, low, high], axis=1)
    def first(part):
        for i in range(4 * part, 4 * part + 4):
            load(i).wait()
        for i in range(4 * part, 4 * part + 4):
            high, low = split(jnp.concatenate([s_buf[i, 0], s_buf[i, 1]], axis=1))
            t = jnp.dot(fyl[...], jnp.concatenate([high, high, low], axis=0), preferred_element_type=F32)
            for h in range(2):
                piece = t[:, 128 * h:128 * h + 128]
                t1s[i, 64 * h:64 * h + 64] = piece[:64]
                t1o[i, 64 * h:64 * h + 64] = piece[64:]

    def swap(part):
        at = pl.ds(4 * part, 4)
        return pltpu.make_async_remote_copy(
            src_ref=t1s.at[at], dst_ref=t1r.at[at], send_sem=ys.at[part], recv_sem=yr.at[part],
            device_id=(gx, other, xi), device_id_type=MESH)

    def second_of(part):
        swap(part).wait_recv()
        for i in range(2):
            n = 4 * part + 2 * i
            t2 = (t1o[n:n + 2] + t1r[n:n + 2]).reshape(256, 128)
            w = jnp.concatenate(split(t2), axis=1)
            q = lax.dot_general(fzl[...], w, NT, preferred_element_type=F32)
            q = q[:128] + q[128:]
            t3[pl.ds(n, 128, stride=16), :] = q[:, :128]
            t3[pl.ds(n + 1, 128, stride=16), :] = q[:, 128:]

    def block_of(part, x, y, number):
        j, h = part[:2]
        at = ((j * 4 + x) * 4 + y) * WIDTH
        if h is None:
            return t3.at[pl.ds(pl.multiple_of(at * 16, 32), number * 16)]
        return t3.reshape(129, 2, 8, 128).at[pl.ds(at, number), h]

    def slot_of(ref, part, at):
        j, h = part[:2]
        if h is None:
            return ref.at[j, at]
        return ref.reshape(*ref.shape[:-2], ref.shape[-2] // 16, 2, 8, 128).at[j, at, :, h]

    def relay(part, way):
        return pltpu.make_async_remote_copy(
            src_ref=block_of(part, opposite, 2 * way, 2 * WIDTH), dst_ref=slot_of(rx1, part, way),
            send_sem=r_s.at[part[2], way], recv_sem=r_r.at[part[2], way],
            device_id=(gx, core, (right, left)[way]), device_id_type=MESH)

    def send_relay(part):
        for way in range(2):
            relay(part, way).start()

    def exchange(part, x, y, slot):
        pltpu.make_async_remote_copy(
            src_ref=block_of(part, x, y, WIDTH), dst_ref=slot_of(rx, part, slot * 4 + yi),
            send_sem=x_s.at[part[2]], recv_sem=x_r.at[part[2]],
            device_id=(zi * 4 + y, core, x), device_id_type=MESH).start()

    def send_plain(part):
        @pl.loop(1, 4)
        def _(d):
            exchange(part, xi, lax.rem(yi + d, 4), 1)

        @pl.loop(0, 2)
        def _(y):
            exchange(part, right, y + 2, 0)
            exchange(part, left, y, 2)

    def send_merged(part):
        for way in range(2):
            relay(part, way).wait_recv()
            to = block_of(part, (right, left)[way], 2 * way, 2 * WIDTH)
            to[...] = to[...] + slot_of(rx1, part, way)[...]

        @pl.loop(0, 2)
        def _(y):
            exchange(part, right, y, 0)
            exchange(part, left, y + 2, 2)

    def spread(j, d):
        block, to = in_column(d)
        return pltpu.make_async_remote_copy(
            src_ref=p.at[j, block], dst_ref=zr.at[j, gx],
            send_sem=z_s.at[j], recv_sem=z_r.at[j], device_id=to, device_id_type=MESH)

    def gather_fx(d):
        y = lax.rem(yi + d, 4)
        return pltpu.make_async_remote_copy(
            src_ref=my_fx, dst_ref=my_fx, send_sem=g_s, recv_sem=g_r,
            device_id=(zi * 4 + y, core, xi), device_id_type=MESH)

    dummy = t3

    def wait(ref, sem):
        pltpu.make_async_copy(ref, ref, sem).wait()

    parts = [(0, 0, 0), (0, 1, 1)] + [(j, None, 1 + j) for j in range(1, CHUNKS)]

    def contract(j):
        add = rx[j, 0:4] + rx[j, 4:8] + rx[j, 8:12]
        turned = pltpu.roll(add.reshape(-1, 128), 64, 1).reshape(add.shape)
        low_half = lax.broadcasted_iota(jnp.int32, (16, 128), 1) < 64
        columns = []
        for q in range(PAIRS):
            c0, c1 = slice(16 * q, 16 * q + 16), slice(16 * (PAIRS + q), 16 * (PAIRS + q) + 16)
            pieces = []
            for y in range(4):
                pieces.append(jnp.where(low_half, add[y, c0], turned[y, c1]))
                pieces.append(jnp.where(low_half, turned[y, c0], add[y, c1]))
            columns.append(jnp.concatenate(pieces, axis=0))
        w = jnp.concatenate(split(jnp.concatenate(columns, axis=1)), axis=0)
        r = jnp.dot(fxl[...], w, preferred_element_type=F32)
        r = r[:128] + r[128:]
        for q in range(PAIRS):
            p[j, :, 4 * q:4 * q + 4] = r[:, 128 * q:128 * q + 128].reshape(planes, 4, 128)

    def total(j):
        w = zr[j, 0:4]
        for z in range(1, zn):
            w = w + zr[j, 4 * z:4 * z + 4]
        for y in range(4):
            turned = pltpu.roll(w[y], 64, 1)
            at = (j * 4 + y) * WIDTH * 4
            fin[at:at + 4 * PAIRS] = w[y]
            fin[at + 4 * PAIRS:at + 8 * PAIRS] = turned

    def do_spread(j):
        contract(j)

        @pl.loop(0, planes - 1)
        def _(i):
            k = i // 4
            z = lax.rem(zn // 2 + (k + 1) // 2 * (1 - 2 * lax.rem(k, 2)) + zn, zn)
            spread(j, 4 * z + 3 - lax.rem(i, 4)).start()

        zr[j, gx] = p[j, gx]

    def await_part(n):
        size = slice(0, 11 * WIDTH * 16 // (2 if n < 2 else 1))
        wait(dummy.at[size], x_r.at[n])

    entered = lambda: pl.semaphore_wait(barrier, 8)
    for part in range(4):
        first(part)
        if part == 0:
            load_z.wait()
            group = 4 * WIDTH
            fz_t = fz_v[...].T
            fzl[...] = stacked(jnp.concatenate(
                [fz_t[32 * x + group * j:32 * x + group * (j + 1)] for j in range(CHUNKS) for x in range(4)], axis=0))
            load_x.wait()
            entered()
            for n in range(part):
                swap(n).start()
            tell_x(0)
            tell_z(1, 1)
        swap(part).start()
        if part == 1:
            @pl.loop(1, 4)
            def _(d):
                gather_fx(d).start()
        if part == 3:
            second_of(0)
            second_of(1)
            send_relay(parts[0])
            pl.semaphore_wait(known.at[0], 2)
            send_plain(parts[0])
    second_of(2)
    second_of(3)
    send_relay(parts[1])
    send_plain(parts[1])
    pl.semaphore_wait(known.at[1], 2)
    tell_z(2, 2)
    rx[0, 4 + yi] = t3[rows(plane * WIDTH * 16, WIDTH * 16)]
    for j in range(1, CHUNKS):
        rx[j, 4 + yi] = t3[rows((j * 16 + plane) * WIDTH * 16, WIDTH * 16)]
    send_merged(parts[0])
    send_relay(parts[2])
    send_merged(parts[1])
    pl.semaphore_wait(known.at[2], 2)
    tell_y(3)
    for j in range(1, CHUNKS):
        send_plain(parts[1 + j])
        if j == 1:
            wait(fxg.at[0:96], g_r)
            fxl[...] = stacked(fxg[...].T)
        if j + 1 < CHUNKS:
            send_relay(parts[2 + j])
        send_merged(parts[1 + j])
    pl.semaphore_wait(known.at[3], 3)
    for j in range(CHUNKS):
        if j == 0:
            await_part(0)
            await_part(1)
        else:
            await_part(j + 1)
        do_spread(j)
    for n in range(4):
        swap(n).wait_send()
    wait(fxg.at[0:96], g_s)
    for n, part in enumerate(parts):
        for way in range(2):
            relay(part, way).wait_send()
        wait(dummy.at[0:11 * WIDTH * 16 // (2 if n < 2 else 1)], x_s.at[n])
    for j in range(CHUNKS):
        wait(zr.at[j, 0:planes - 1], z_r.at[j])
        total(j)
    for a in range(4):
        out[a] = fin[pl.ds(a, 32, stride=4), :][:, :64]

    for j in range(CHUNKS):
        wait(zr.at[j, 0:planes - 1], z_s.at[j])


def body(zn, snapshot, factor_x, factor_y, factor_z):
    anywhere = pl.BlockSpec(memory_space=pl.ANY)
    dma = pltpu.SemaphoreType.DMA
    core = pl.pallas_call(
        functools.partial(kernel, zn),
        out_shape=pltpu.VMEM((4, 32, 64), F32),
        in_specs=[anywhere] * 4,
        out_specs=pl.BlockSpec(memory_space=pltpu.VMEM),
        scratch_shapes=[
            pltpu.VMEM((16, 2, 256, 128), F32),
            pltpu.VMEM((256, 128), F32),
            pltpu.VMEM((128, 128), F32),
            pltpu.VMEM((128, 128), F32),
            pltpu.VMEM((128, 256), F32),
            pltpu.VMEM((128, 768), BF16),
            pltpu.VMEM((256, 256), BF16),
            pltpu.VMEM((256, 256), BF16),
            pltpu.VMEM((16, 128, 128), F32),
            pltpu.VMEM((16, 128, 128), F32),
            pltpu.VMEM((16, 128, 128), F32),
            pltpu.VMEM((2064, 128), F32),
            pltpu.VMEM((CHUNKS, 12, WIDTH * 16, 128), F32),
            pltpu.VMEM((CHUNKS, 2, WIDTH * 32, 128), F32),
            pltpu.VMEM((CHUNKS, 4 * zn, 4 * PAIRS, 128), F32),
            pltpu.VMEM((CHUNKS, 4 * zn, 4 * PAIRS, 128), F32),
            pltpu.VMEM((136, 128), F32),
            dma((16,)), dma((3,)), dma((4,)), dma((4,)),
            dma((1 + CHUNKS, 2)), dma((1 + CHUNKS, 2)), dma((1 + CHUNKS,)), dma((1 + CHUNKS,)), dma((CHUNKS,)), dma((CHUNKS,)), dma, dma,
            pltpu.SemaphoreType.REGULAR((4,)),
        ],
        compiler_params=pltpu.CompilerParams(
            collective_id=0, has_side_effects=True, vmem_limit_bytes=40 * 1024 * 1024
        ),
    )(*(pltpu.with_memory_space_constraint(a, pltpu.HBM) for a in (snapshot.reshape(2, 16, 256, 128), factor_x, factor_y, factor_z)))
    return core.transpose(0, 2, 1)


def solution(mesh):
    return jax.shard_map(
        functools.partial(body, mesh.shape["gx"] // 4),
        mesh=mesh,
        in_specs=(P("gx", "gy", "gz"), P("gx", None), P("gy", None), P("gz", None)),
        out_specs=P("gx", "gy", "gz"),
        check_vma=False,
    )
```

```python
import functools

import jax
import jax.numpy as jnp
from jax import lax
from jax.experimental import pallas as pl
from jax.experimental.pallas import tpu as pltpu
from jax.sharding import PartitionSpec as P

MESH = pl.DeviceIdType.MESH
F32, BF16 = jnp.float32, jnp.bfloat16
NT = (((1,), (1,)), ((), ()))
CHUNKS = 2
WIDTH = 8 // CHUNKS
PAIRS = WIDTH // 2


def split(value):
    high = value.astype(BF16)
    return high, (value - high.astype(F32)).astype(BF16)


def rows(start, size):
    return pl.ds(pl.multiple_of(start, 8), size)


def stacked(factor_t):
    high, low = split(factor_t)
    top = jnp.concatenate([high, high], axis=1)
    return jnp.concatenate([top, jnp.concatenate([low, jnp.zeros_like(low)], axis=1)], axis=0)


def kernel(
    zn, snap, fx, fy, fz, out,
    s_buf, fy_v, fz_v, fxg, ft, fyl, fzl, fxl, t1s, t1o, t1r, t3, rx, rx1, p, zr, fin,
    s_sem, f_sem, ys, yr, r_s, r_r, x_s, x_r, z_s, z_r, g_s, g_r, known,
):
    gx, core, xi = lax.axis_index("gx"), lax.axis_index("gy"), lax.axis_index("gz")
    zi, yi = gx // 4, lax.rem(gx, 4)
    other = 1 - core
    plane = xi * 4 + yi
    planes = 4 * zn

    right, opposite, left = lax.rem(xi + 1, 4), lax.rem(xi + 2, 4), lax.rem(xi + 3, 4)

    def in_column(d):
        z, y = lax.rem(zi + d // 4, zn), lax.rem(yi + lax.rem(d, 4), 4)
        return z * 4 + y, (z * 4 + y, core, xi)

    def load(i):
        return pltpu.make_async_copy(snap.at[:, i], s_buf.at[i], s_sem.at[i])

    load_y = pltpu.make_async_copy(fy, fy_v, f_sem.at[0])
    load_z = pltpu.make_async_copy(fz, fz_v, f_sem.at[1])
    my_fx = fxg.at[rows(yi * 32, 32)]
    load_x = pltpu.make_async_copy(fx, my_fx, f_sem.at[2])
    load_y.start()
    load_z.start()
    load_x.start()

    @pl.loop(0, 16)
    def _(i):
        load(i).start()

    barrier = pltpu.get_barrier_semaphore()
    pl.semaphore_signal(barrier, inc=1, device_id=(gx, other, xi), device_id_type=MESH)

    for x in (left, right):
        pl.semaphore_signal(barrier, inc=1, device_id=(gx, core, x), device_id_type=MESH)

    @pl.loop(1, 4)
    def _(d):
        pl.semaphore_signal(barrier, inc=1, device_id=in_column(d)[1], device_id_type=MESH)

    for d in (1, zn - 1):
        pl.semaphore_signal(barrier, inc=1, device_id=in_column(4 * d)[1], device_id_type=MESH)

    def tell_x(stage):
        for x in (left, right):
            pl.semaphore_signal(known.at[stage], inc=1, device_id=(gx, core, x), device_id_type=MESH)

    def tell_y(stage):
        @pl.loop(1, 4)
        def _(d):
            pl.semaphore_signal(known.at[stage], inc=1, device_id=in_column(d)[1], device_id_type=MESH)

    def tell_z(stage, distance):
        for d in (distance, zn - distance):
            pl.semaphore_signal(known.at[stage], inc=1, device_id=in_column(4 * d)[1], device_id_type=MESH)

    load_y.wait()
    ft[...] = fy_v[...].T
    high, low = split(jnp.concatenate([ft[rows(other * 64, 64)], ft[rows(core * 64, 64)]], axis=0))
    fyl[...] = jnp.concatenate([high, low, high], axis=1)
    def first(part):
        for i in range(4 * part, 4 * part + 4):
            load(i).wait()
        for i in range(4 * part, 4 * part + 4):
            high, low = split(jnp.concatenate([s_buf[i, 0], s_buf[i, 1]], axis=1))
            t = jnp.dot(fyl[...], jnp.concatenate([high, high, low], axis=0), preferred_element_type=F32)
            for h in range(2):
                piece = t[:, 128 * h:128 * h + 128]
                t1s[i, 64 * h:64 * h + 64] = piece[:64]
                t1o[i, 64 * h:64 * h + 64] = piece[64:]

    def swap(part):
        at = pl.ds(4 * part, 4)
        return pltpu.make_async_remote_copy(
            src_ref=t1s.at[at], dst_ref=t1r.at[at], send_sem=ys.at[part], recv_sem=yr.at[part],
            device_id=(gx, other, xi), device_id_type=MESH)

    def second_of(part):
        swap(part).wait_recv()
        for i in range(2):
            n = 4 * part + 2 * i
            t2 = (t1o[n:n + 2] + t1r[n:n + 2]).reshape(256, 128)
            w = jnp.concatenate(split(t2), axis=1)
            q = lax.dot_general(fzl[...], w, NT, preferred_element_type=F32)
            q = q[:128] + q[128:]
            t3[pl.ds(n, 128, stride=16), :] = q[:, :128]
            t3[pl.ds(n + 1, 128, stride=16), :] = q[:, 128:]

    def block_of(part, x, y, number):
        j, h = part[:2]
        at = ((j * 4 + x) * 4 + y) * WIDTH
        if h is None:
            return t3.at[pl.ds(pl.multiple_of(at * 16, 32), number * 16)]
        return t3.reshape(129, 2, 8, 128).at[pl.ds(at, number), h]

    def slot_of(ref, part, at):
        j, h = part[:2]
        if h is None:
            return ref.at[j, at]
        return ref.reshape(*ref.shape[:-2], ref.shape[-2] // 16, 2, 8, 128).at[j, at, :, h]

    def relay(part, way):
        return pltpu.make_async_remote_copy(
            src_ref=block_of(part, opposite, 2 * way, 2 * WIDTH), dst_ref=slot_of(rx1, part, way),
            send_sem=r_s.at[part[2], way], recv_sem=r_r.at[part[2], way],
            device_id=(gx, core, (right, left)[way]), device_id_type=MESH)

    def send_relay(part):
        for way in range(2):
            relay(part, way).start()

    def exchange(part, x, y, slot):
        pltpu.make_async_remote_copy(
            src_ref=block_of(part, x, y, WIDTH), dst_ref=slot_of(rx, part, slot * 4 + yi),
            send_sem=x_s.at[part[2]], recv_sem=x_r.at[part[2]],
            device_id=(zi * 4 + y, core, x), device_id_type=MESH).start()

    def send_plain(part):
        @pl.loop(0, 2)
        def _(y):
            exchange(part, right, y + 2, 0)
            exchange(part, left, y, 2)

        @pl.loop(1, 4)
        def _(d):
            exchange(part, xi, lax.rem(yi + d, 4), 1)

    def send_merged(part):
        for way in range(2):
            relay(part, way).wait_recv()
            to = block_of(part, (right, left)[way], 2 * way, 2 * WIDTH)
            to[...] = to[...] + slot_of(rx1, part, way)[...]

        @pl.loop(0, 2)
        def _(y):
            exchange(part, right, y, 0)
            exchange(part, left, y + 2, 2)

    def spread(j, d):
        block, to = in_column(d)
        return pltpu.make_async_remote_copy(
            src_ref=p.at[j, block], dst_ref=zr.at[j, gx],
            send_sem=z_s.at[j], recv_sem=z_r.at[j], device_id=to, device_id_type=MESH)

    def gather_fx(d):
        y = lax.rem(yi + d, 4)
        return pltpu.make_async_remote_copy(
            src_ref=my_fx, dst_ref=my_fx, send_sem=g_s, recv_sem=g_r,
            device_id=(zi * 4 + y, core, xi), device_id_type=MESH)

    dummy = t3

    def wait(ref, sem):
        pltpu.make_async_copy(ref, ref, sem).wait()

    parts = [(0, 0, 0), (0, 1, 1)] + [(j, None, 1 + j) for j in range(1, CHUNKS)]

    def contract(j):
        add = rx[j, 0:4] + rx[j, 4:8] + rx[j, 8:12]
        turned = pltpu.roll(add.reshape(-1, 128), 64, 1).reshape(add.shape)
        low_half = lax.broadcasted_iota(jnp.int32, (16, 128), 1) < 64
        columns = []
        for q in range(PAIRS):
            c0, c1 = slice(16 * q, 16 * q + 16), slice(16 * (PAIRS + q), 16 * (PAIRS + q) + 16)
            pieces = []
            for y in range(4):
                pieces.append(jnp.where(low_half, add[y, c0], turned[y, c1]))
                pieces.append(jnp.where(low_half, turned[y, c0], add[y, c1]))
            columns.append(jnp.concatenate(pieces, axis=0))
        w = jnp.concatenate(split(jnp.concatenate(columns, axis=1)), axis=0)
        r = jnp.dot(fxl[...], w, preferred_element_type=F32)
        r = r[:128] + r[128:]
        for q in range(PAIRS):
            p[j, :, 4 * q:4 * q + 4] = r[:, 128 * q:128 * q + 128].reshape(planes, 4, 128)

    def total(j):
        w = zr[j, 0:4]
        for z in range(1, zn):
            w = w + zr[j, 4 * z:4 * z + 4]
        for y in range(4):
            turned = pltpu.roll(w[y], 64, 1)
            at = (j * 4 + y) * WIDTH * 4
            fin[at:at + 4 * PAIRS] = w[y]
            fin[at + 4 * PAIRS:at + 8 * PAIRS] = turned

    def do_spread(j):
        contract(j)

        @pl.loop(0, planes - 1)
        def _(i):
            k = i // 4
            z = lax.rem(zn // 2 + (k + 1) // 2 * (1 - 2 * lax.rem(k, 2)) + zn, zn)
            spread(j, 4 * z + 3 - lax.rem(i, 4)).start()

        zr[j, gx] = p[j, gx]

    def await_part(n):
        size = slice(0, 11 * WIDTH * 16 // (2 if n < 2 else 1))
        wait(dummy.at[size], x_r.at[n])

    entered = lambda: pl.semaphore_wait(barrier, 8)
    for part in range(4):
        first(part)
        if part == 0:
            load_z.wait()
            group = 4 * WIDTH
            fz_t = fz_v[...].T
            fzl[...] = stacked(jnp.concatenate(
                [fz_t[32 * x + group * j:32 * x + group * (j + 1)] for j in range(CHUNKS) for x in range(4)], axis=0))
            load_x.wait()
            entered()
            for n in range(part):
                swap(n).start()
            tell_x(0)
            tell_z(1, 1)
        swap(part).start()
        if part == 1:
            @pl.loop(1, 4)
            def _(d):
                gather_fx(d).start()
        if part == 3:
            second_of(0)
            second_of(1)
            send_relay(parts[0])
            pl.semaphore_wait(known.at[0], 2)
            send_plain(parts[0])
    second_of(2)
    second_of(3)
    send_relay(parts[1])
    send_plain(parts[1])
    pl.semaphore_wait(known.at[1], 2)
    tell_z(2, 2)
    rx[0, 4 + yi] = t3[rows(plane * WIDTH * 16, WIDTH * 16)]
    for j in range(1, CHUNKS):
        rx[j, 4 + yi] = t3[rows((j * 16 + plane) * WIDTH * 16, WIDTH * 16)]
    send_merged(parts[0])
    send_relay(parts[2])
    send_merged(parts[1])
    pl.semaphore_wait(known.at[2], 2)
    tell_y(3)
    for j in range(1, CHUNKS):
        send_plain(parts[1 + j])
        if j == 1:
            wait(fxg.at[0:96], g_r)
            fxl[...] = stacked(fxg[...].T)
        if j + 1 < CHUNKS:
            send_relay(parts[2 + j])
        send_merged(parts[1 + j])
    pl.semaphore_wait(known.at[3], 3)
    for j in range(CHUNKS):
        if j == 0:
            await_part(0)
            await_part(1)
        else:
            await_part(j + 1)
        do_spread(j)
    for n in range(4):
        swap(n).wait_send()
    wait(fxg.at[0:96], g_s)
    for n, part in enumerate(parts):
        for way in range(2):
            relay(part, way).wait_send()
        wait(dummy.at[0:11 * WIDTH * 16 // (2 if n < 2 else 1)], x_s.at[n])
    for j in range(CHUNKS):
        wait(zr.at[j, 0:planes - 1], z_r.at[j])
        total(j)
    for a in range(4):
        out[a] = fin[pl.ds(a, 32, stride=4), :][:, :64]

    for j in range(CHUNKS):
        wait(zr.at[j, 0:planes - 1], z_s.at[j])


def body(zn, snapshot, factor_x, factor_y, factor_z):
    anywhere = pl.BlockSpec(memory_space=pl.ANY)
    dma = pltpu.SemaphoreType.DMA
    core = pl.pallas_call(
        functools.partial(kernel, zn),
        out_shape=pltpu.VMEM((4, 32, 64), F32),
        in_specs=[anywhere] * 4,
        out_specs=pl.BlockSpec(memory_space=pltpu.VMEM),
        scratch_shapes=[
            pltpu.VMEM((16, 2, 256, 128), F32),
            pltpu.VMEM((256, 128), F32),
            pltpu.VMEM((128, 128), F32),
            pltpu.VMEM((128, 128), F32),
            pltpu.VMEM((128, 256), F32),
            pltpu.VMEM((128, 768), BF16),
            pltpu.VMEM((256, 256), BF16),
            pltpu.VMEM((256, 256), BF16),
            pltpu.VMEM((16, 128, 128), F32),
            pltpu.VMEM((16, 128, 128), F32),
            pltpu.VMEM((16, 128, 128), F32),
            pltpu.VMEM((2064, 128), F32),
            pltpu.VMEM((CHUNKS, 12, WIDTH * 16, 128), F32),
            pltpu.VMEM((CHUNKS, 2, WIDTH * 32, 128), F32),
            pltpu.VMEM((CHUNKS, 4 * zn, 4 * PAIRS, 128), F32),
            pltpu.VMEM((CHUNKS, 4 * zn, 4 * PAIRS, 128), F32),
            pltpu.VMEM((136, 128), F32),
            dma((16,)), dma((3,)), dma((4,)), dma((4,)),
            dma((1 + CHUNKS, 2)), dma((1 + CHUNKS, 2)), dma((1 + CHUNKS,)), dma((1 + CHUNKS,)), dma((CHUNKS,)), dma((CHUNKS,)), dma, dma,
            pltpu.SemaphoreType.REGULAR((4,)),
        ],
        compiler_params=pltpu.CompilerParams(
            collective_id=0, has_side_effects=True, vmem_limit_bytes=40 * 1024 * 1024
        ),
    )(*(pltpu.with_memory_space_constraint(a, pltpu.HBM) for a in (snapshot.reshape(2, 16, 256, 128), factor_x, factor_y, factor_z)))
    return core.transpose(0, 2, 1)


def solution(mesh):
    return jax.shard_map(
        functools.partial(body, mesh.shape["gx"] // 4),
        mesh=mesh,
        in_specs=(P("gx", "gy", "gz"), P("gx", None), P("gy", None), P("gz", None)),
        out_specs=P("gx", "gy", "gz"),
        check_vma=False,
    )
```
